512 devices in a mesh: enc: 128 (over y, z, core), agg: 4 (over x).
Axes of the slice: x: 4, y: 4, z: 16, core: 2. Of those that a mesh axis runs over, the one named last changes fastest.
Arguments:
- features: bfloat16 [18432, 4, 2048], P('enc'), may hold values from -6 to 6
- tile_slide: int32 [18432, 1], P('enc'), may hold values from 0 to 127; in each aligned block of 144 rows (0 to 143, 144 to 287, ...) at most 2 rows name the same one
- tile_pos: int32 [18432], P('enc'), may hold values from 0 to 255
- slide_owner: int32 [128], replicated, may hold values from 0 to 127, each once
- slide_label: int32 [128], replicated, may hold values from 0 to 31
- enc_weight: bfloat16 [2048, 768], P(None, 'agg'), may hold values from -0.125 to 0.125
- enc_bias: float32 [768], P('agg'), may hold values from -3 to 3
- norm_gain: float32 [768], replicated, may hold values from 0.1 to 1.9
- qkv_weight: bfloat16 [768, 2304], P('enc'), may hold values from -0.21875 to 0.21875
- out_weight: bfloat16 [768, 768], P('enc'), may hold values from -0.21875 to 0.21875
- cls_weight: float32 [768, 32], replicated, may hold values from -0.6 to 0.6
Outputs:
- owner_logits: float32 [128, 32], P('enc')
- enc_grad: float32 [2048, 768], P(None, 'agg')
- bias_grad: float32 [768], P('agg')
The draws below stay inside these ranges and needn't reach their ends.
Inputs may be any that keep to these rules, and one draw needn't show every extreme that they name: `tile_slide`: in each aligned block of 144 tiles (the tiles of one index of enc) no slide has more than 2 tiles, and some slide has exactly that many in some block; every slide has a tile. `slide_owner`: each index of enc owns exactly one slide.
All inputs are finite; a program needn't handle non-finite values.
Results may differ from the reference program's by a relative error of at most 0.012.
Values may be sent and summed in bfloat16 or wider, within the bound.
No kernel may reach another device: no remote copies, remote signals or barrier semaphores. Data moves between devices by JAX's collectives and lax.ppermute only.
A program may use at most 64 MiB of HBM per device.

```python
import math
import jax
import jax.numpy as jnp
import numpy as np
from jax import lax

CH = 2048
POS = 4
EMB = 768
HEADS = 12
CLASSES = 32
GRID = 256
TILE_DEV = 144
HD = 64
SEND_MOST = 2
SLIDES = 128
TILES = 18432


def set_ends(entries, stream_key, smallest, largest):
    shape = entries.shape
    spot = [jax.random.randint(jax.random.fold_in(stream_key, axis), (), 0, shape[axis]) for axis in range(len(shape))]
    entries = entries.at[tuple(spot)].set(smallest)
    longest = shape.index(max(shape))
    spot[longest] = (spot[longest] + 1) % shape[longest]
    return entries.at[tuple(spot)].set(largest)


def steps_of(key, extent, split, low, high):
    def one(axis_at, blocks):
        steps = jax.random.uniform(jax.random.fold_in(jax.random.fold_in(key, 6), axis_at), (blocks,), jnp.float32, low / len(split), high / len(split))
        return jnp.repeat(jnp.exp(steps), extent[axis_at] // blocks).reshape((-1,) + (1,) * (len(extent) - axis_at - 1))

    loudness = one(*split[0])
    for cut in split[1:]:
        loudness = loudness * one(*cut)
    return loudness


def routed_block(stream_key, own, number, rows, number_of, top, bound, skew):
    order = jax.random.permutation(stream_key, number_of)
    packed, usual = load_shares(number_of, rows * top, bound, skew, True), load_shares(number_of, rows * top, bound, skew, False)
    places = jnp.arange(number_of)

    def named(sizes, offset_by):
        used = int((sizes > 0).sum())
        fixed = max(1, used // 4)
        passed = fixed + (places - fixed + offset_by * (used - fixed)) % max(1, number_of - fixed)
        return jnp.zeros((number_of,), jnp.int32).at[order[jnp.where(places < fixed, places, passed)]].set(jnp.asarray(sizes, jnp.int32))

    sizes = jnp.where(number % 4 == 0, named(packed, number // 4), named(usual, number - number // 4 - 1))
    mixed = jax.random.permutation(jax.random.fold_in(own, 3), number_of)
    donor, sink = mixed[0:number_of // 2 * 2:2], mixed[1:number_of // 2 * 2:2]
    room = jnp.minimum(sizes[donor] - 1, bound - sizes[sink]) // 2
    room = jnp.where((donor == order[0]) | (sink == order[0]) | (sizes[sink] == 0), 0, jnp.maximum(room, 0))
    passed = jax.random.randint(jax.random.fold_in(own, 4), (number_of // 2,), 0, 1 << 20) % (room + 1)
    sizes = sizes.at[donor].add(-passed).at[sink].add(passed)
    labels = jnp.searchsorted(jnp.cumsum(sizes), jnp.arange(rows * top), side="right").astype(jnp.int32)
    listing = labels.reshape(top, rows).T
    listing = listing[jax.random.permutation(jax.random.fold_in(own, 1), rows)]
    offset_by = jax.random.randint(jax.random.fold_in(own, 2), (rows, 1), 0, top)
    return jnp.take_along_axis(listing, (jnp.arange(top)[None, :] + offset_by) % top, axis=1)


def load_shares(number_of, total, bound, slope, full):
    weights = [(1 << 20) // math.isqrt(grade ** slope) + 1 for grade in range(1, number_of + 1)]
    largest = bound if full else min(bound, max(-(-total // number_of), total * weights[0] // sum(weights)))
    least = 1 if total - largest >= number_of - 1 else 0
    given, rest = [largest] + [least] * (number_of - 1), total - largest - least * (number_of - 1)
    while rest > 0:
        movable = [i for i in range(1, number_of) if given[i] < largest] or [i for i in range(1, number_of) if given[i] < bound]
        whole, budget = sum([weights[i] for i in movable]), rest
        for i in movable:
            more = min(bound - given[i], max(1, budget * weights[i] // whole), rest)
            given[i] = given[i] + more
            rest = rest - more
    return np.array(given)


def gaussian(own_key, dims, spread, bound, cuts=(), kind=jnp.bfloat16):
    values = spread * jax.random.normal(own_key, dims, jnp.float32)
    if cuts:
        values = values * steps_of(own_key, dims, cuts, -0.22, 0.18)
    return jnp.clip(values, -bound, bound).astype(kind)


def setup_inputs(seed: int = 0) -> dict:
    arg_keys = jax.random.split(jax.random.key(seed), 12)
    features = gaussian(arg_keys[0], (TILES, POS, CH), 1.0, 6.0, ((0, 128),))
    tile_slide_keys = jax.random.split(jax.random.fold_in(arg_keys[1], 1), TILES // TILE_DEV)
    tile_slide_turns = jax.random.permutation(jax.random.fold_in(arg_keys[1], 3), TILES // TILE_DEV)
    tile_slide = jax.vmap(lambda own, number: routed_block(jax.random.fold_in(arg_keys[1], 2), own, number, TILE_DEV, SLIDES, 1, SEND_MOST, 2))(tile_slide_keys, tile_slide_turns).reshape((TILES, 1))
    tile_pos = set_ends(jax.random.randint(arg_keys[2], (TILES,), 0, GRID), jax.random.fold_in(arg_keys[2], 1), 0, GRID - 1).astype(jnp.int32)
    slide_owner = jax.random.permutation(arg_keys[3], SLIDES).astype(jnp.int32)
    slide_label = set_ends(jax.random.randint(arg_keys[4], (SLIDES,), 0, CLASSES), jax.random.fold_in(arg_keys[4], 1), 0, CLASSES - 1).astype(jnp.int32)
    enc_weight = gaussian(arg_keys[5], (CH, EMB), CH ** -0.5, 0.125, ((1, 4),))
    enc_bias = gaussian(arg_keys[6], (EMB,), 0.5, 3.0, ((0, 4),), jnp.float32)
    norm_gain = jnp.clip(1.0 + 0.18 * jax.random.normal(arg_keys[7], (EMB,), jnp.float32), 0.1, 1.9)
    qkv_weight = gaussian(arg_keys[8], (EMB, 3 * EMB), EMB ** -0.5, 0.21875, ((0, 128),))
    out_weight = gaussian(arg_keys[9], (EMB, EMB), EMB ** -0.5, 0.21875, ((0, 128),))
    cls_weight = gaussian(arg_keys[10], (EMB, CLASSES), 0.1, 0.6, (), jnp.float32)
    return {"features": features, "tile_slide": tile_slide, "tile_pos": tile_pos, "slide_owner": slide_owner, "slide_label": slide_label, "enc_weight": enc_weight, "enc_bias": enc_bias, "norm_gain": norm_gain, "qkv_weight": qkv_weight, "out_weight": out_weight, "cls_weight": cls_weight}


eps = 1e-05

def rounded(values):
    return lax.optimization_barrier(values.astype(jnp.bfloat16)).astype(jnp.float32)

def dilation_table():
    head_ids = jnp.arange(HEADS, dtype=jnp.int32)
    group_ids = head_ids % 3
    segment_len = jnp.left_shift(jnp.int32(64), group_ids)
    stride_len = jnp.left_shift(jnp.int32(1), group_ids)
    return (segment_len, stride_len)

def visible_mask(query_pos, key_pos, segment_len, stride_len):
    seg_col = segment_len[:, None, None]
    str_col = stride_len[:, None, None]
    same_seg = query_pos[None, :, None] // seg_col == key_pos[None, None, :] // seg_col
    same_res = query_pos[None, :, None] % str_col == key_pos[None, None, :] % str_col
    return same_seg & same_res

def layer_norm(row_values, norm_gain):
    centred = row_values - lax.optimization_barrier(jnp.mean(row_values, axis=-1, keepdims=True))
    variance = lax.optimization_barrier(jnp.mean(centred * centred, axis=-1, keepdims=True))
    inv_std = lax.rsqrt(variance + eps)
    normed = centred * inv_std
    return (normed, inv_std, (normed * norm_gain).astype(jnp.bfloat16))

def norm_backward(grad_normed, normed, inv_std, norm_gain):
    scaled = grad_normed * norm_gain
    return inv_std * (scaled - lax.optimization_barrier(jnp.mean(scaled, axis=-1, keepdims=True)) - normed * lax.optimization_barrier(jnp.mean(scaled * normed, axis=-1, keepdims=True)))

def reference(features, tile_slide, tile_pos, slide_owner, slide_label, enc_weight, enc_bias, norm_gain, qkv_weight, out_weight, cls_weight):
    tile_total = features.shape[0]
    flattened = features.reshape(tile_total * POS, CH)
    preact = jnp.dot(flattened, enc_weight, preferred_element_type=jnp.float32).reshape(tile_total, POS, EMB) + enc_bias
    tile_rows = lax.optimization_barrier(jnp.mean(jnp.maximum(preact, 0.0), axis=1)).astype(jnp.bfloat16)
    row_values = tile_rows.astype(jnp.float32)
    normed, inv_std, normed_in = layer_norm(row_values, norm_gain)
    qkv_all = jnp.dot(normed_in, qkv_weight, preferred_element_type=jnp.float32)
    score_scale = HD ** (-0.5)
    query_heads = rounded(qkv_all[:, :EMB] * score_scale).reshape(tile_total, HEADS, HD)
    key_heads = rounded(qkv_all[:, EMB:2 * EMB]).reshape(tile_total, HEADS, HD)
    value_heads = rounded(qkv_all[:, 2 * EMB:]).reshape(tile_total, HEADS, HD)
    slide_ids = tile_slide[:, 0]
    segment_len, stride_len = dilation_table()
    block_rows = math.gcd(tile_total, 256)
    block_count = tile_total // block_rows
    block_starts = jnp.arange(block_count, dtype=jnp.int32) * block_rows

    def block_weights(start):
        query_block = lax.dynamic_slice_in_dim(query_heads, start, block_rows, 0)
        query_pos = lax.dynamic_slice_in_dim(tile_pos, start, block_rows, 0)
        query_slide = lax.dynamic_slice_in_dim(slide_ids, start, block_rows, 0)
        scores = jnp.einsum('qhd,khd->hqk', query_block, key_heads)
        visible = visible_mask(query_pos, tile_pos, segment_len, stride_len) & (query_slide[:, None] == slide_ids[None, :])[None]
        masked = jnp.where(visible, scores, -1e+30)
        row_max = lax.optimization_barrier(jnp.max(masked, axis=-1, keepdims=True))
        weights = jnp.where(visible, jnp.exp(masked - row_max), 0.0)
        return (weights / lax.optimization_barrier(jnp.sum(weights, axis=-1, keepdims=True)), query_block)

    def forward_block(start):
        weights, query_block = block_weights(start)
        mixed = jnp.einsum('hqk,khd->qhd', rounded(weights), value_heads)
        return mixed.reshape(block_rows, EMB).astype(jnp.bfloat16)
    attended = lax.map(forward_block, block_starts).reshape(tile_total, EMB)
    projected = jnp.dot(attended, out_weight, preferred_element_type=jnp.float32)
    outputs = row_values + projected
    counts = jax.ops.segment_sum(jnp.ones((tile_total,), jnp.float32), slide_ids, num_segments=SLIDES)
    pooled = jax.ops.segment_sum(outputs, slide_ids, num_segments=SLIDES) / counts[:, None]
    logits = jnp.dot(pooled, cls_weight, precision=lax.Precision.HIGHEST)
    class_probs = jax.nn.softmax(logits, axis=-1)
    grad_logits = class_probs - jax.nn.one_hot(slide_label, CLASSES, dtype=jnp.float32)
    grad_pooled = jnp.dot(grad_logits, cls_weight.T, precision=lax.Precision.HIGHEST) / counts[:, None]
    grad_mixed_slide = jnp.dot(grad_pooled.astype(jnp.bfloat16), out_weight.T, preferred_element_type=jnp.float32)
    grad_heads = rounded(grad_mixed_slide)[slide_ids].reshape(tile_total, HEADS, HD)

    def backward_step(carry, start):
        key_acc, value_acc = carry
        weights, query_block = block_weights(start)
        probs_in = rounded(weights)
        grad_block = lax.dynamic_slice_in_dim(grad_heads, start, block_rows, 0)
        grad_att = jnp.einsum('qhd,khd->hqk', grad_block, value_heads)
        grad_scores = rounded(weights * (grad_att - lax.optimization_barrier(jnp.sum(weights * grad_att, axis=-1, keepdims=True))))
        grad_query = jnp.einsum('hqk,khd->qhd', grad_scores, key_heads) * score_scale
        key_acc = key_acc + jnp.einsum('hqk,qhd->khd', grad_scores, query_block)
        value_acc = value_acc + jnp.einsum('hqk,qhd->khd', probs_in, grad_block)
        return ((key_acc, value_acc), grad_query.reshape(block_rows, EMB))
    zero_heads = jnp.zeros((tile_total, HEADS, HD), jnp.float32)
    (grad_key, grad_value), grad_query = lax.scan(backward_step, (zero_heads, zero_heads), block_starts)
    grad_qkv = jnp.concatenate([grad_query.reshape(tile_total, EMB), grad_key.reshape(tile_total, EMB), grad_value.reshape(tile_total, EMB)], axis=1).astype(jnp.bfloat16)
    grad_normed = lax.dot_general(grad_qkv, qkv_weight, (((1,), (1,)), ((), ())), preferred_element_type=jnp.float32)
    tile_grads = rounded(grad_pooled[slide_ids] + norm_backward(grad_normed, normed, inv_std, norm_gain))
    grad_preact = jnp.where(preact > 0, tile_grads[:, None, :] / POS, 0.0).astype(jnp.bfloat16)
    enc_grad = lax.dot_general(flattened, grad_preact.reshape(tile_total * POS, EMB), (((0,), (0,)), ((), ())), preferred_element_type=jnp.float32)
    bias_grad = lax.optimization_barrier(jnp.sum(grad_preact.astype(jnp.float32), axis=(0, 1)))
    owner_logits = jnp.zeros((SLIDES, CLASSES), jnp.float32).at[slide_owner].set(logits)
    return (owner_logits, enc_grad, bias_grad)
```

```python
import jax
import jax.numpy as jnp
from jax import lax
from jax.experimental import pallas as pl
from jax.experimental.pallas import tpu as pltpu
from jax.sharding import Mesh, PartitionSpec as P

POS = 4
HEADS = 12
CLASSES = 32
HD = 64
SLOTS = 2
BLOCK = 256
ENC = ("y", "z", "c")
NEAR = ("y", "c")
eps = 1e-05

bf16 = jnp.bfloat16
f32 = jnp.float32
EXACT = lax.Precision.HIGHEST


def across(lhs, rhs, dims, precision=None):
    return lax.dot_general(
        lhs, rhs, ((dims[:1], dims[1:]), ((), ())), precision=precision, preferred_element_type=f32
    )


def normed_parts(rows_ref, cols):
    parts = [rows_ref[part, :, :cols].astype(f32) for part in range(rows_ref.shape[0])]
    width = cols * len(parts)
    mean = sum(jnp.sum(part, axis=1, keepdims=True) for part in parts) / width
    centred = [part - mean for part in parts]
    variance = sum(jnp.sum(part * part, axis=1, keepdims=True) for part in centred) / width
    inv_std = lax.rsqrt(variance + eps)
    return parts, [part * inv_std for part in centred], inv_std


def forward_kernel(place_ref, rows_ref, weight_ref, gain_ref, cls_ref, logits_ref, att_ref, qkv_ref):
    groups, slots, _ = rows_ref.shape
    cols = gain_ref.shape[2]
    parts, normed, _ = normed_parts(rows_ref, cols)
    qkv = jnp.zeros((slots, 3 * cols), f32)
    for part in range(groups):
        normed_in = (normed[part] * gain_ref[part]).astype(bf16)
        block = weight_ref[part * cols : (part + 1) * cols, : 3 * cols]
        qkv = qkv + across(normed_in, block, (1, 0))
    column = lax.broadcasted_iota(jnp.int32, (slots, 3 * cols), 1)
    qkv = jnp.where(column < cols, qkv * HD ** (-0.5), qkv).astype(bf16)
    qkv_ref[...] = qkv
    tags = rows_ref[0, :, cols : cols + 1].astype(f32)
    count = jnp.sum(tags, axis=0, keepdims=True) * 0.0 + jnp.sum(
        (tags > 0).astype(f32), axis=0, keepdims=True
    )
    down = lax.broadcasted_iota(jnp.int32, (slots, slots), 0)
    along = lax.broadcasted_iota(jnp.int32, (slots, slots), 1)
    tag_row = jnp.sum(jnp.where(down == along, tags, 0.0), axis=0, keepdims=True)
    query_pos = tags.astype(jnp.int32) - 1
    key_pos = tag_row.astype(jnp.int32) - 1
    wc_pair = weight_ref[pl.ds(pl.multiple_of(place_ref[0] * cols, 16), cols), 3 * cols :].astype(f32)
    wc = wc_pair[:, :CLASSES] + wc_pair[:, CLASSES : 2 * CLASSES]
    total = jnp.zeros((1, CLASSES), f32)
    for head in range(cols // HD):
        group = head % 3
        low = (1 << group) - 1
        query_key = ((query_pos >> (6 + group)) << group) + (query_pos & low)
        key_key = ((key_pos >> (6 + group)) << group) + (key_pos & low)
        query_key = jnp.where(query_pos < 0, -1, query_key)
        key_key = jnp.where(key_pos < 0, -2, key_key)
        visible = query_key == key_key
        first = head * HD
        scores = across(
            qkv[:, first : first + HD], qkv[:, cols + first : cols + first + HD], (1, 1)
        )
        masked = jnp.where(visible, scores, -1e30)
        row_max = jnp.max(masked, axis=1, keepdims=True)
        weights = jnp.where(visible, jnp.exp(masked - row_max), 0.0)
        row_total = jnp.sum(weights, axis=1, keepdims=True)
        att = weights / jnp.where(row_total > 0, row_total, 1.0)
        att_ref[head] = att
        att_total = jnp.sum(att.astype(bf16).astype(f32), axis=0, keepdims=True)
        values = qkv[:, 2 * cols + first : 2 * cols + first + HD].astype(f32)
        mixed_total = across(att_total, values, (1, 0), EXACT)
        total = total + across(mixed_total, wc[first : first + HD], (1, 0), EXACT)
    for part in range(groups):
        row_sum = jnp.sum(parts[part], axis=0, keepdims=True) * (1.0 / groups)
        total = total + across(row_sum, cls_ref[part], (1, 1), EXACT)
    logits_ref[...] = total / count


def backward_kernel(
    place_ref,
    logits_ref,
    owner_ref,
    label_ref,
    rows_ref,
    weight_ref,
    gain_ref,
    cls_ref,
    att_ref,
    qkv_ref,
    grad_ref,
):
    groups, slots, _ = rows_ref.shape
    cols = gain_ref.shape[2]
    _, normed, inv_std = normed_parts(rows_ref, cols)
    tags = rows_ref[0, :, cols : cols + 1].astype(f32)
    live = (tags > 0).astype(f32)
    count = jnp.sum(live, axis=0, keepdims=True)
    logits = logits_ref[...]
    scaled = jnp.exp(logits - jnp.max(logits, axis=1, keepdims=True))
    class_probs = scaled / jnp.sum(scaled, axis=1, keepdims=True)
    mine = owner_ref[...] == place_ref[1]
    my_label = jnp.sum(jnp.where(mine, label_ref[...], 0).astype(f32), axis=1, keepdims=True)
    class_ids = lax.broadcasted_iota(jnp.int32, (1, CLASSES), 1).astype(f32)
    grad_logits = (class_probs - (class_ids == my_label).astype(f32)) / count
    wc_pair = weight_ref[pl.ds(pl.multiple_of(place_ref[0] * cols, 16), cols), 3 * cols :].astype(f32)
    wc = wc_pair[:, :CLASSES] + wc_pair[:, CLASSES : 2 * CLASSES]
    grad_mixed = across(grad_logits, wc, (1, 1), EXACT).astype(bf16)
    qkv = qkv_ref[...]
    grad_q, grad_k, grad_v = [], [], []
    for head in range(cols // HD):
        first = head * HD
        att = att_ref[head]
        queries = qkv[:, first : first + HD]
        keys = qkv[:, cols + first : cols + first + HD]
        values = qkv[:, 2 * cols + first : 2 * cols + first + HD]
        head_grad = grad_mixed[:, first : first + HD]
        grad_att = across(head_grad, values, (1, 1))
        expected = jnp.sum(att * grad_att, axis=1, keepdims=True)
        grad_scores = (att * (grad_att - expected)).astype(bf16)
        grad_q.append(across(grad_scores, keys, (1, 0)) * HD ** (-0.5))
        grad_k.append(across(grad_scores, queries, (0, 0)))
        spread = jnp.broadcast_to(head_grad, (slots, HD))
        grad_v.append(across(att.astype(bf16), spread, (0, 0)))
    grad_qkv = jnp.concatenate(grad_q + grad_k + grad_v, axis=1).astype(bf16)
    scaled_parts = []
    for part in range(groups):
        block = weight_ref[part * cols : (part + 1) * cols, : 3 * cols]
        scaled_parts.append(across(grad_qkv, block, (1, 1)) * gain_ref[part])
    width = cols * groups
    mean = sum(jnp.sum(e, axis=1, keepdims=True) for e in scaled_parts) / width
    slope = (
        sum(jnp.sum(e * n, axis=1, keepdims=True) for e, n in zip(scaled_parts, normed)) / width
    )
    for part in range(groups):
        pooled = across(grad_logits, cls_ref[part], (1, 0), EXACT) * (1.0 / groups)
        grad = inv_std * (scaled_parts[part] - mean - normed[part] * slope)
        grad_ref[part] = (live * pooled + grad).astype(bf16)


def on_device(
    features,
    tile_slide,
    tile_pos,
    slide_owner,
    slide_label,
    enc_weight,
    enc_bias,
    norm_gain,
    qkv_weight,
    out_weight,
    cls_weight,
):
    enc_count = lax.axis_size(ENC)
    far_count = lax.axis_size("z")
    near_count = lax.axis_size(NEAR)
    groups = lax.axis_size("x")
    tile_count, _, channels = features.shape
    cols = enc_weight.shape[1]
    emb = cols * groups
    slide_count = slide_owner.shape[0]
    slot_total = enc_count * SLOTS
    group_at = lax.axis_index("x")
    owner_at = lax.axis_index(ENC)

    with jax.named_scope("weights"):
        wc_rows = jnp.dot(out_weight.astype(f32), cls_weight, precision=EXACT)
        wc_high = wc_rows.astype(bf16)
        wc_low = (wc_rows - wc_high.astype(f32)).astype(bf16)
        picked = [
            lax.dynamic_slice_in_dim(qkv_weight, part * emb + group_at * cols, cols, 1)
            for part in range(3)
        ]
        weight_rows = jnp.concatenate(picked + [wc_high, wc_low], axis=1)
        far_rows = lax.all_gather(weight_rows, "z", axis=0, tiled=False)
        near_rows = lax.all_gather(far_rows, NEAR, axis=0, tiled=False)
        held = near_rows.shape[2:]
        weights = (
            near_rows.reshape((lax.axis_size("y"), lax.axis_size("c"), far_count) + held)
            .transpose(0, 2, 1, 3, 4)
            .reshape(emb, held[1])
        )

    with jax.named_scope("encode"):
        flattened = features.reshape(tile_count * POS, channels)
        preact = (
            jnp.dot(flattened, enc_weight, preferred_element_type=f32).reshape(
                tile_count, POS, cols
            )
            + enc_bias
        )
        tile_rows = jnp.mean(jnp.maximum(preact, 0.0), axis=1).astype(bf16)

    with jax.named_scope("dispatch"):
        slide_ids = tile_slide[:, 0]
        slide_range = jnp.arange(slide_count, dtype=jnp.int32)
        owners = jnp.sum(
            jnp.where(slide_ids[:, None] == slide_range[None, :], slide_owner[None, :], 0), axis=1
        )
        tile_range = jnp.arange(tile_count, dtype=jnp.int32)
        earlier = tile_range[None, :] < tile_range[:, None]
        slot_rank = jnp.sum(
            ((slide_ids[:, None] == slide_ids[None, :]) & earlier).astype(jnp.int32), axis=1
        )
        target = owners * SLOTS + slot_rank
        placing = (jnp.arange(slot_total, dtype=jnp.int32)[:, None] == target[None, :]).astype(bf16)
        tagged = jnp.concatenate(
            [
                tile_rows,
                (tile_pos + 1).astype(bf16)[:, None],
                jnp.zeros((tile_count, BLOCK - cols - 1), bf16),
            ],
            axis=1,
        )
        send_rows = (
            jnp.dot(placing, tagged, preferred_element_type=f32)
            .astype(bf16)
            .reshape(enc_count, SLOTS, BLOCK)
        )
        slot_rows = lax.all_to_all(send_rows, ENC, split_axis=0, concat_axis=0, tiled=True)
        rows = lax.all_gather(slot_rows.reshape(slot_total, BLOCK), "x", axis=0, tiled=False)

    with jax.named_scope("attend"):
        place = jnp.stack([group_at, owner_at]).astype(jnp.int32)
        gain = norm_gain.reshape(groups, 1, cols)
        cls_parts = cls_weight.T.reshape(CLASSES, groups, cols).transpose(1, 0, 2)
        in_smem = pl.BlockSpec(memory_space=pltpu.SMEM)
        in_vmem = pl.BlockSpec(memory_space=pltpu.VMEM)
        part_logits, att, qkv = pl.pallas_call(
            forward_kernel,
            out_shape=(
                jax.ShapeDtypeStruct((1, CLASSES), f32),
                jax.ShapeDtypeStruct((cols // HD, slot_total, slot_total), f32),
                jax.ShapeDtypeStruct((slot_total, 3 * cols), bf16),
            ),
            in_specs=[in_smem] + [in_vmem] * 4,
            out_specs=(in_vmem,) * 3,
            compiler_params=pltpu.CompilerParams(vmem_limit_bytes=32 << 20),
            name="forward",
        )(place, rows, weights, gain, cls_parts)
        logits = lax.psum(part_logits, "x")
        grad_parts = pl.pallas_call(
            backward_kernel,
            out_shape=jax.ShapeDtypeStruct((groups, slot_total, cols), bf16),
            in_specs=[in_smem] + [in_vmem] * 9,
            out_specs=in_vmem,
            compiler_params=pltpu.CompilerParams(vmem_limit_bytes=32 << 20),
            name="backward",
        )(
            place,
            logits,
            slide_owner[None, :],
            slide_label[None, :],
            rows,
            weights,
            gain,
            cls_parts,
            att,
            qkv,
        )

    with jax.named_scope("give_back"):
        from_groups = lax.all_to_all(grad_parts, "x", split_axis=0, concat_axis=0, tiled=True)
        grad_rows = jnp.sum(from_groups.astype(f32), axis=0).astype(bf16)
        back_rows = lax.all_to_all(
            grad_rows.reshape(enc_count, SLOTS, cols), ENC, split_axis=0, concat_axis=0, tiled=True
        ).reshape(slot_total, cols)

    with jax.named_scope("encoder_grad"):
        tile_grads = across(placing, back_rows, (0, 0))
        grad_preact = jnp.where(preact > 0, tile_grads[:, None, :] / POS, 0.0).astype(bf16)
        grad_preact = grad_preact.reshape(tile_count * POS, cols)
        grad_part = across(grad_preact, flattened, (0, 0)).astype(bf16)
        bias_part = jnp.sum(grad_preact.astype(f32), axis=0).astype(bf16)

    with jax.named_scope("reduce"):
        near_rows = cols // near_count
        lanes = channels // far_count
        bias_lanes = jnp.broadcast_to(
            bias_part.reshape(near_count, near_rows, 1), (near_count, near_rows, lanes)
        )
        near_send = jnp.concatenate(
            [grad_part.reshape(near_count, near_rows, channels), bias_lanes], axis=2
        )
        near_sum = jnp.sum(
            lax.all_to_all(near_send, NEAR, split_axis=0, concat_axis=0, tiled=True).astype(f32),
            axis=0,
        )
        far_send = (
            near_sum[:, :channels].reshape(near_rows, far_count, lanes).transpose(1, 0, 2)
        ).astype(bf16)
        bias_row = jnp.pad(near_sum[:, channels], (0, lanes - near_rows)).astype(bf16)
        far_send = jnp.concatenate(
            [far_send, jnp.broadcast_to(bias_row[None, None, :], (far_count, 8, lanes))], axis=1
        )
        far_sum = jnp.sum(
            lax.all_to_all(far_send, "z", split_axis=0, concat_axis=0, tiled=True).astype(f32),
            axis=0,
        ).astype(bf16)
        far_all = lax.all_gather(far_sum, "z", axis=0, tiled=False)
        all_parts = lax.all_gather(far_all, NEAR, axis=0, tiled=False).astype(f32)
        enc_grad = (
            all_parts[:, :, :near_rows].transpose(0, 2, 1, 3).reshape(cols, channels).T
        )
        bias_grad = all_parts[:, 0, near_rows, :near_rows].reshape(cols)
    return (logits, enc_grad, bias_grad)


def solution(mesh):
    enc_count, groups = mesh.devices.shape
    split = Mesh(mesh.devices.reshape(4, enc_count // 8, 2, groups), ("y", "z", "c", "x"))
    return jax.shard_map(
        on_device,
        mesh=split,
        in_specs=(
            P(ENC, None, None),
            P(ENC, None),
            P(ENC),
            P(),
            P(),
            P(None, "x"),
            P("x"),
            P(),
            P(ENC, None),
            P(ENC, None),
            P(),
        ),
        out_specs=(P(ENC, None), P(None, "x"), P("x")),
        check_vma=False,
    )
```

```python
import jax
import jax.numpy as jnp
from jax import lax
from jax.experimental import pallas as pl
from jax.experimental.pallas import tpu as pltpu
from jax.sharding import Mesh, PartitionSpec as P

POS = 4
HEADS = 12
CLASSES = 32
HD = 64
SLOTS = 2
BLOCK = 256
ENC = ("y", "z", "c")
NEAR = ("y", "c")
eps = 1e-05

bf16 = jnp.bfloat16
f32 = jnp.float32
EXACT = lax.Precision.HIGHEST


def across(lhs, rhs, dims, precision=None):
    return lax.dot_general(
        lhs, rhs, ((dims[:1], dims[1:]), ((), ())), precision=precision, preferred_element_type=f32
    )


def gather_far(block, far_count):
    copies = jnp.broadcast_to(block[None], (far_count,) + block.shape)
    return lax.all_to_all(copies, "z", split_axis=0, concat_axis=0, tiled=True)


def normed_parts(rows_ref, cols):
    parts = [rows_ref[part, :, :cols].astype(f32) for part in range(rows_ref.shape[0])]
    width = cols * len(parts)
    mean = sum(jnp.sum(part, axis=1, keepdims=True) for part in parts) / width
    centred = [part - mean for part in parts]
    variance = sum(jnp.sum(part * part, axis=1, keepdims=True) for part in centred) / width
    inv_std = lax.rsqrt(variance + eps)
    return parts, [part * inv_std for part in centred], inv_std


def forward_kernel(place_ref, rows_ref, weight_ref, gain_ref, cls_ref, logits_ref, att_ref, qkv_ref):
    groups, slots, _ = rows_ref.shape
    cols = gain_ref.shape[2]
    parts, normed, _ = normed_parts(rows_ref, cols)
    qkv = jnp.zeros((slots, 3 * cols), f32)
    for part in range(groups):
        normed_in = (normed[part] * gain_ref[part]).astype(bf16)
        block = weight_ref[part * cols : (part + 1) * cols, : 3 * cols]
        qkv = qkv + across(normed_in, block, (1, 0))
    column = lax.broadcasted_iota(jnp.int32, (slots, 3 * cols), 1)
    qkv = jnp.where(column < cols, qkv * HD ** (-0.5), qkv).astype(bf16)
    qkv_ref[...] = qkv
    tags = rows_ref[0, :, cols : cols + 1].astype(f32)
    count = jnp.sum(tags, axis=0, keepdims=True) * 0.0 + jnp.sum(
        (tags > 0).astype(f32), axis=0, keepdims=True
    )
    down = lax.broadcasted_iota(jnp.int32, (slots, slots), 0)
    along = lax.broadcasted_iota(jnp.int32, (slots, slots), 1)
    tag_row = jnp.sum(jnp.where(down == along, tags, 0.0), axis=0, keepdims=True)
    query_pos = tags.astype(jnp.int32) - 1
    key_pos = tag_row.astype(jnp.int32) - 1
    wc_pair = weight_ref[pl.ds(pl.multiple_of(place_ref[0] * cols, 16), cols), 3 * cols :].astype(f32)
    wc = wc_pair[:, :CLASSES] + wc_pair[:, CLASSES : 2 * CLASSES]
    total = jnp.zeros((1, CLASSES), f32)
    for head in range(cols // HD):
        group = head % 3
        low = (1 << group) - 1
        query_key = ((query_pos >> (6 + group)) << group) + (query_pos & low)
        key_key = ((key_pos >> (6 + group)) << group) + (key_pos & low)
        query_key = jnp.where(query_pos < 0, -1, query_key)
        key_key = jnp.where(key_pos < 0, -2, key_key)
        visible = query_key == key_key
        first = head * HD
        scores = across(
            qkv[:, first : first + HD], qkv[:, cols + first : cols + first + HD], (1, 1)
        )
        masked = jnp.where(visible, scores, -1e30)
        row_max = jnp.max(masked, axis=1, keepdims=True)
        weights = jnp.where(visible, jnp.exp(masked - row_max), 0.0)
        row_total = jnp.sum(weights, axis=1, keepdims=True)
        att = weights / jnp.where(row_total > 0, row_total, 1.0)
        att_ref[head] = att
        att_total = jnp.sum(att.astype(bf16).astype(f32), axis=0, keepdims=True)
        values = qkv[:, 2 * cols + first : 2 * cols + first + HD].astype(f32)
        mixed_total = across(att_total, values, (1, 0), EXACT)
        total = total + across(mixed_total, wc[first : first + HD], (1, 0), EXACT)
    for part in range(groups):
        row_sum = jnp.sum(parts[part], axis=0, keepdims=True) * (1.0 / groups)
        total = total + across(row_sum, cls_ref[part], (1, 1), EXACT)
    logits_ref[...] = total / count


def backward_kernel(
    place_ref,
    part_logits_ref,
    owner_ref,
    label_ref,
    rows_ref,
    weight_ref,
    gain_ref,
    cls_ref,
    att_ref,
    qkv_ref,
    logits_ref,
    grad_ref,
):
    groups, slots, _ = rows_ref.shape
    cols = gain_ref.shape[2]
    _, normed, inv_std = normed_parts(rows_ref, cols)
    tags = rows_ref[0, :, cols : cols + 1].astype(f32)
    live = (tags > 0).astype(f32)
    count = jnp.sum(live, axis=0, keepdims=True)
    logits = sum(part_logits_ref[part] for part in range(groups))
    logits_ref[...] = logits
    scaled = jnp.exp(logits - jnp.max(logits, axis=1, keepdims=True))
    class_probs = scaled / jnp.sum(scaled, axis=1, keepdims=True)
    mine = owner_ref[...] == place_ref[1]
    my_label = jnp.sum(jnp.where(mine, label_ref[...], 0).astype(f32), axis=1, keepdims=True)
    class_ids = lax.broadcasted_iota(jnp.int32, (1, CLASSES), 1).astype(f32)
    grad_logits = (class_probs - (class_ids == my_label).astype(f32)) / count
    wc_pair = weight_ref[pl.ds(pl.multiple_of(place_ref[0] * cols, 16), cols), 3 * cols :].astype(f32)
    wc = wc_pair[:, :CLASSES] + wc_pair[:, CLASSES : 2 * CLASSES]
    grad_mixed = across(grad_logits, wc, (1, 1), EXACT).astype(bf16)
    qkv = qkv_ref[...]
    grad_q, grad_k, grad_v = [], [], []
    for head in range(cols // HD):
        first = head * HD
        att = att_ref[head]
        queries = qkv[:, first : first + HD]
        keys = qkv[:, cols + first : cols + first + HD]
        values = qkv[:, 2 * cols + first : 2 * cols + first + HD]
        head_grad = grad_mixed[:, first : first + HD]
        grad_att = across(head_grad, values, (1, 1))
        expected = jnp.sum(att * grad_att, axis=1, keepdims=True)
        grad_scores = (att * (grad_att - expected)).astype(bf16)
        grad_q.append(across(grad_scores, keys, (1, 0)) * HD ** (-0.5))
        grad_k.append(across(grad_scores, queries, (0, 0)))
        spread = jnp.broadcast_to(head_grad, (slots, HD))
        grad_v.append(across(att.astype(bf16), spread, (0, 0)))
    grad_qkv = jnp.concatenate(grad_q + grad_k + grad_v, axis=1).astype(bf16)
    scaled_parts = []
    for part in range(groups):
        block = weight_ref[part * cols : (part + 1) * cols, : 3 * cols]
        scaled_parts.append(across(grad_qkv, block, (1, 1)) * gain_ref[part])
    width = cols * groups
    mean = sum(jnp.sum(e, axis=1, keepdims=True) for e in scaled_parts) / width
    slope = (
        sum(jnp.sum(e * n, axis=1, keepdims=True) for e, n in zip(scaled_parts, normed)) / width
    )
    for part in range(groups):
        pooled = across(grad_logits, cls_ref[part], (1, 0), EXACT) * (1.0 / groups)
        grad = inv_std * (scaled_parts[part] - mean - normed[part] * slope)
        grad_ref[part] = (live * pooled + grad).astype(bf16)


def on_device(
    features,
    tile_slide,
    tile_pos,
    slide_owner,
    slide_label,
    enc_weight,
    enc_bias,
    norm_gain,
    qkv_weight,
    out_weight,
    cls_weight,
):
    far_count = lax.axis_size("z")
    near_count = lax.axis_size(NEAR)
    groups = lax.axis_size("x")
    tile_count, _, channels = features.shape
    cols = enc_weight.shape[1]
    emb = cols * groups
    slide_count = slide_owner.shape[0]
    slot_total = far_count * near_count * SLOTS
    group_at = lax.axis_index("x")
    owner_at = lax.axis_index(ENC)

    with jax.named_scope("weights"):
        wc_rows = jnp.dot(out_weight.astype(f32), cls_weight, precision=EXACT)
        wc_high = wc_rows.astype(bf16)
        wc_low = (wc_rows - wc_high.astype(f32)).astype(bf16)
        picked = [
            lax.dynamic_slice_in_dim(qkv_weight, part * emb + group_at * cols, cols, 1)
            for part in range(3)
        ]
        weight_rows = jnp.concatenate(picked + [wc_high, wc_low], axis=1)
        far_rows = gather_far(weight_rows, far_count)
        line_rows = lax.all_gather(far_rows, "y", axis=0)
        held = lax.all_gather(line_rows, "c", axis=0)
        weights = held.transpose(1, 2, 0, 3, 4).reshape(emb, held.shape[4])

    with jax.named_scope("encode"):
        flattened = features.reshape(tile_count * POS, channels)
        preact = (
            jnp.dot(flattened, enc_weight, preferred_element_type=f32).reshape(
                tile_count, POS, cols
            )
            + enc_bias
        )
        tile_rows = jnp.mean(jnp.maximum(preact, 0.0), axis=1).astype(bf16)

    with jax.named_scope("dispatch"):
        slide_ids = tile_slide[:, 0]
        slide_range = jnp.arange(slide_count, dtype=jnp.int32)
        owners = jnp.sum(
            jnp.where(slide_ids[:, None] == slide_range[None, :], slide_owner[None, :], 0), axis=1
        )
        tile_range = jnp.arange(tile_count, dtype=jnp.int32)
        earlier = tile_range[None, :] < tile_range[:, None]
        slot_rank = jnp.sum(
            ((slide_ids[:, None] == slide_ids[None, :]) & earlier).astype(jnp.int32), axis=1
        )
        near_owner = owners // (2 * far_count) * 2 + owners % 2
        far_owner = owners // 2 % far_count
        target = (far_owner * near_count + near_owner) * SLOTS + slot_rank
        placing = (jnp.arange(slot_total, dtype=jnp.int32)[:, None] == target[None, :]).astype(bf16)
        unread = BLOCK - cols - 1
        tagged = jnp.concatenate(
            [
                tile_rows,
                (tile_pos + 1).astype(bf16)[:, None],
                jnp.broadcast_to(far_rows[:1, 0, :unread], (tile_count, unread)),
            ],
            axis=1,
        )
        send_rows = (
            jnp.dot(placing, tagged, preferred_element_type=f32)
            .astype(bf16)
            .reshape(far_count, near_count * SLOTS, BLOCK)
        )
        far_in = lax.all_to_all(send_rows, "z", split_axis=0, concat_axis=0, tiled=True)
        lane = lax.broadcasted_iota(jnp.int32, far_in.shape, 2)
        far_in = jnp.where(lane > cols, line_rows[0, :1, :1, :BLOCK], far_in)
        by_near = far_in.reshape(far_count, near_count, SLOTS, BLOCK).transpose(1, 0, 2, 3)
        send_near = jnp.broadcast_to(
            by_near.reshape(1, near_count, far_count * SLOTS, BLOCK),
            (groups, near_count, far_count * SLOTS, BLOCK),
        ).reshape(groups * near_count, far_count * SLOTS, BLOCK)
        rows = lax.all_to_all(
            send_near, ("x",) + NEAR, split_axis=0, concat_axis=0, tiled=True
        ).reshape(groups, slot_total, BLOCK)

    with jax.named_scope("attend"):
        place = jnp.stack([group_at, owner_at]).astype(jnp.int32)
        gain = norm_gain.reshape(groups, 1, cols)
        cls_parts = cls_weight.T.reshape(CLASSES, groups, cols).transpose(1, 0, 2)
        in_smem = pl.BlockSpec(memory_space=pltpu.SMEM)
        in_vmem = pl.BlockSpec(memory_space=pltpu.VMEM)
        part_logits, att, qkv = pl.pallas_call(
            forward_kernel,
            out_shape=(
                jax.ShapeDtypeStruct((1, CLASSES), f32),
                jax.ShapeDtypeStruct((cols // HD, slot_total, slot_total), f32),
                jax.ShapeDtypeStruct((slot_total, 3 * cols), bf16),
            ),
            in_specs=[in_smem] + [in_vmem] * 4,
            out_specs=(in_vmem,) * 3,
            compiler_params=pltpu.CompilerParams(vmem_limit_bytes=32 << 20),
            name="forward",
        )(place, rows, weights, gain, cls_parts)
        all_logits = lax.all_gather(part_logits, "x", axis=0)
        logits, grad_parts = pl.pallas_call(
            backward_kernel,
            out_shape=(
                jax.ShapeDtypeStruct((1, CLASSES), f32),
                jax.ShapeDtypeStruct((groups, slot_total, cols), bf16),
            ),
            in_specs=[in_smem] + [in_vmem] * 9,
            out_specs=(in_vmem,) * 2,
            compiler_params=pltpu.CompilerParams(vmem_limit_bytes=32 << 20),
            name="backward",
        )(
            place,
            all_logits,
            slide_owner[None, :],
            slide_label[None, :],
            rows,
            weights,
            gain,
            cls_parts,
            att,
            qkv,
        )

    with jax.named_scope("give_back"):
        from_near = lax.all_to_all(
            grad_parts.reshape(groups * near_count, far_count * SLOTS, cols),
            ("x",) + NEAR,
            split_axis=0,
            concat_axis=0,
            tiled=True,
        ).reshape(groups, near_count, far_count, SLOTS, cols)
        grad_rows = jnp.sum(from_near.astype(f32), axis=0).astype(bf16)
        back_rows = lax.all_to_all(
            grad_rows.transpose(1, 0, 2, 3).reshape(far_count, near_count * SLOTS, cols),
            "z",
            split_axis=0,
            concat_axis=0,
            tiled=True,
        ).reshape(slot_total, cols)

    with jax.named_scope("encoder_grad"):
        tile_grads = across(placing, back_rows, (0, 0))
        grad_preact = jnp.where(preact > 0, tile_grads[:, None, :] / POS, 0.0).astype(bf16)
        grad_preact = grad_preact.reshape(tile_count * POS, cols)
        grad_part = across(grad_preact, flattened, (0, 0)).astype(bf16)
        bias_part = jnp.sum(grad_preact.astype(f32), axis=0).astype(bf16)

    with jax.named_scope("reduce"):
        core_at = lax.axis_index("c")
        near_rows = cols // near_count
        core_rows = cols // 2
        lanes = channels // far_count
        both = jnp.concatenate(
            [grad_part, jnp.broadcast_to(bias_part[:, None], (cols, lanes))], axis=1
        )
        kept = lax.dynamic_slice_in_dim(both, core_at * core_rows, core_rows, 0)
        sent = lax.dynamic_slice_in_dim(both, (1 - core_at) * core_rows, core_rows, 0)
        other = lax.ppermute(sent, "c", [(0, 1), (1, 0)])
        core_sum = (kept.astype(f32) + other.astype(f32)).astype(bf16)
        near_sum = jnp.sum(
            lax.all_to_all(
                core_sum.reshape(core_rows // near_rows, near_rows, channels + lanes),
                "y",
                split_axis=0,
                concat_axis=0,
                tiled=True,
            ).astype(f32),
            axis=0,
        )
        far_send = (
            near_sum[:, :channels].reshape(near_rows, far_count, lanes).transpose(1, 0, 2)
        ).astype(bf16)
        bias_row = jnp.pad(near_sum[:, channels], (0, lanes - near_rows)).astype(bf16)
        far_send = jnp.concatenate(
            [far_send, jnp.broadcast_to(bias_row[None, None, :], (far_count, 1, lanes))], axis=1
        )
        far_sum = jnp.sum(
            lax.all_to_all(far_send, "z", split_axis=0, concat_axis=0, tiled=True).astype(f32),
            axis=0,
        ).astype(bf16)
        far_all = gather_far(far_sum, far_count)
        all_parts = lax.all_gather(lax.all_gather(far_all, "y", axis=0), "c", axis=0).astype(f32)
        enc_grad = (
            all_parts[:, :, :, :near_rows].transpose(0, 1, 3, 2, 4).reshape(cols, channels).T
        )
        bias_grad = all_parts[:, :, 0, near_rows, :near_rows].reshape(cols)
    return (logits, enc_grad, bias_grad)


def solution(mesh):
    enc_count, groups = mesh.devices.shape
    split = Mesh(mesh.devices.reshape(4, enc_count // 8, 2, groups), ("y", "z", "c", "x"))
    return jax.shard_map(
        on_device,
        mesh=split,
        in_specs=(
            P(ENC, None, None),
            P(ENC, None),
            P(ENC),
            P(),
            P(),
            P(None, "x"),
            P("x"),
            P(),
            P(ENC, None),
            P(ENC, None),
            P(),
        ),
        out_specs=(P(ENC, None), P(None, "x"), P("x")),
        check_vma=False,
    )
```

```python
import functools

import jax
import jax.numpy as jnp
from jax import lax
from jax.experimental import pallas as pl
from jax.experimental.pallas import tpu as pltpu
from jax.sharding import Mesh, PartitionSpec as P

POS = 4
HEADS = 12
CLASSES = 32
HD = 64
SLOTS = 2
BLOCK = 256
LANES = 128
FAR = ("zh", "zl")
ENC = ("y", "zh", "zl", "c")
NEAR = ("y", "c")
PLANE = ("y", "zl")
eps = 1e-05

bf16 = jnp.bfloat16
f32 = jnp.float32
EXACT = lax.Precision.HIGHEST


def across(lhs, rhs, dims, precision=None):
    return lax.dot_general(
        lhs, rhs, ((dims[:1], dims[1:]), ((), ())), precision=precision, preferred_element_type=f32
    )


def swap(blocks, axes):
    return lax.all_to_all(blocks, axes, split_axis=0, concat_axis=0, tiled=True)


def gather_copies(block, axes):
    return swap(jnp.broadcast_to(block[None], (lax.axis_size(axes),) + block.shape), axes)


def sum_blocks(blocks, axes):
    return jnp.sum(swap(blocks, axes).astype(f32), axis=0).astype(bf16)


def normed_parts(rows_ref, cols):
    parts = [rows_ref[part, :, :cols].astype(f32) for part in range(rows_ref.shape[0])]
    width = cols * len(parts)
    mean = sum(jnp.sum(part, axis=1, keepdims=True) for part in parts) / width
    centred = [part - mean for part in parts]
    variance = sum(jnp.sum(part * part, axis=1, keepdims=True) for part in centred) / width
    inv_std = lax.rsqrt(variance + eps)
    return parts, [part * inv_std for part in centred], inv_std


def forward_kernel(
    own_rows, place_ref, rows_ref, weight_ref, gain_ref, cls_ref, logits_ref, att_ref, qkv_ref
):
    groups, slots, _ = rows_ref.shape
    cols = gain_ref.shape[2]
    parts, normed, _ = normed_parts(rows_ref, cols)
    size = weight_ref.shape[2] // (-(-(3 * cols + 2 * CLASSES) // LANES))
    order = held_order(own_rows, cols)
    qkv = 0.0
    for part in range(groups):
        normed_in = (normed[part] * gain_ref[part]).astype(bf16)
        normed_in = across(normed_in, order, (1, 0)).astype(bf16)
        block = jnp.concatenate(weight_block(weight_ref, part, size), axis=1)
        qkv = qkv + across(normed_in, block, (1, 0))
    qkv = qkv[:, : 3 * cols]
    column = lax.broadcasted_iota(jnp.int32, (slots, 3 * cols), 1)
    qkv = jnp.where(column < cols, qkv * HD ** (-0.5), qkv).astype(bf16)
    qkv_ref[...] = qkv
    tags = rows_ref[0, :, cols : cols + 1].astype(f32)
    count = jnp.sum(tags, axis=0, keepdims=True) * 0.0 + jnp.sum(
        (tags > 0).astype(f32), axis=0, keepdims=True
    )
    down = lax.broadcasted_iota(jnp.int32, (slots, slots), 0)
    along = lax.broadcasted_iota(jnp.int32, (slots, slots), 1)
    tag_row = jnp.sum(jnp.where(down == along, tags, 0.0), axis=0, keepdims=True)
    query_pos = tags.astype(jnp.int32) - 1
    key_pos = tag_row.astype(jnp.int32) - 1
    wc = class_block(weight_ref, order, place_ref[0], size, cols)
    total = jnp.zeros((1, CLASSES), f32)
    for head in range(cols // HD):
        group = head % 3
        low = (1 << group) - 1
        query_key = ((query_pos >> (6 + group)) << group) + (query_pos & low)
        key_key = ((key_pos >> (6 + group)) << group) + (key_pos & low)
        query_key = jnp.where(query_pos < 0, -1, query_key)
        key_key = jnp.where(key_pos < 0, -2, key_key)
        visible = query_key == key_key
        first = head * HD
        scores = across(
            qkv[:, first : first + HD], qkv[:, cols + first : cols + first + HD], (1, 1)
        )
        masked = jnp.where(visible, scores, -1e30)
        row_max = jnp.max(masked, axis=1, keepdims=True)
        weights = jnp.where(visible, jnp.exp(masked - row_max), 0.0)
        row_total = jnp.sum(weights, axis=1, keepdims=True)
        att = weights / jnp.where(row_total > 0, row_total, 1.0)
        att_ref[head] = att
        att_total = jnp.sum(att.astype(bf16).astype(f32), axis=0, keepdims=True)
        values = qkv[:, 2 * cols + first : 2 * cols + first + HD].astype(f32)
        mixed_total = across(att_total, values, (1, 0), EXACT)
        total = total + across(mixed_total, wc[first : first + HD], (1, 0), EXACT)
    for part in range(groups):
        row_sum = jnp.sum(parts[part], axis=0, keepdims=True) * (1.0 / groups)
        total = total + across(row_sum, cls_ref[part], (1, 1), EXACT)
    logits_ref[...] = total / count


def backward_kernel(
    own_rows,
    place_ref,
    part_logits_ref,
    owner_ref,
    label_ref,
    rows_ref,
    weight_ref,
    gain_ref,
    cls_ref,
    att_ref,
    qkv_ref,
    logits_ref,
    grad_ref,
):
    groups, slots, _ = rows_ref.shape
    cols = gain_ref.shape[2]
    _, normed, inv_std = normed_parts(rows_ref, cols)
    tags = rows_ref[0, :, cols : cols + 1].astype(f32)
    live = (tags > 0).astype(f32)
    count = jnp.sum(live, axis=0, keepdims=True)
    logits = sum(part_logits_ref[part] for part in range(groups))
    logits_ref[...] = logits
    scaled = jnp.exp(logits - jnp.max(logits, axis=1, keepdims=True))
    class_probs = scaled / jnp.sum(scaled, axis=1, keepdims=True)
    mine = owner_ref[...] == place_ref[1]
    my_label = jnp.sum(jnp.where(mine, label_ref[...], 0).astype(f32), axis=1, keepdims=True)
    class_ids = lax.broadcasted_iota(jnp.int32, (1, CLASSES), 1).astype(f32)
    grad_logits = (class_probs - (class_ids == my_label).astype(f32)) / count
    size = weight_ref.shape[2] // (-(-(3 * cols + 2 * CLASSES) // LANES))
    order = held_order(own_rows, cols)
    wc = class_block(weight_ref, order, place_ref[0], size, cols)
    grad_mixed = across(grad_logits, wc, (1, 1), EXACT).astype(bf16)
    qkv = qkv_ref[...]
    grad_q, grad_k, grad_v = [], [], []
    for head in range(cols // HD):
        first = head * HD
        att = att_ref[head]
        queries = qkv[:, first : first + HD]
        keys = qkv[:, cols + first : cols + first + HD]
        values = qkv[:, 2 * cols + first : 2 * cols + first + HD]
        head_grad = grad_mixed[:, first : first + HD]
        grad_att = across(head_grad, values, (1, 1))
        expected = jnp.sum(att * grad_att, axis=1, keepdims=True)
        grad_scores = (att * (grad_att - expected)).astype(bf16)
        grad_q.append(across(grad_scores, keys, (1, 0)) * HD ** (-0.5))
        grad_k.append(across(grad_scores, queries, (0, 0)))
        spread = jnp.broadcast_to(head_grad, (slots, HD))
        grad_v.append(across(att.astype(bf16), spread, (0, 0)))
    unused = jnp.zeros((slots, 2 * CLASSES), f32)
    grad_qkv = jnp.concatenate(grad_q + grad_k + grad_v + [unused], axis=1).astype(bf16)
    scaled_parts = []
    for part in range(groups):
        block = jnp.concatenate(weight_block(weight_ref, part, size), axis=1)
        grad_normed = across(grad_qkv, block, (1, 1))
        high = grad_normed.astype(bf16)
        low = (grad_normed - high.astype(f32)).astype(bf16)
        grad_normed = across(high, order, (1, 1)) + across(low, order, (1, 1))
        scaled_parts.append(grad_normed * gain_ref[part])
    width = cols * groups
    mean = sum(jnp.sum(e, axis=1, keepdims=True) for e in scaled_parts) / width
    slope = (
        sum(jnp.sum(e * n, axis=1, keepdims=True) for e, n in zip(scaled_parts, normed)) / width
    )
    for part in range(groups):
        pooled = across(grad_logits, cls_ref[part], (1, 0), EXACT) * (1.0 / groups)
        grad = inv_std * (scaled_parts[part] - mean - normed[part] * slope)
        grad_ref[part] = (live * pooled + grad).astype(bf16)


def as_column(row):
    size = row.shape[1]
    down = lax.broadcasted_iota(jnp.int32, (size, size), 0)
    along = lax.broadcasted_iota(jnp.int32, (size, size), 1)
    return jnp.sum(jnp.where(down == along, row, 0.0), axis=1, keepdims=True)


def held_rows(rows):
    return (rows + 8) // 8 * 8


def fold_rows(rows, count):
    blocks = rows.reshape(count, 2 * 8, rows.shape[1])
    rest = jnp.concatenate([blocks[:, :8, LANES:], blocks[:, 8:, LANES:]], axis=2)
    return jnp.concatenate([blocks[:, :, :LANES], rest], axis=1)


def unfold_rows(blocks):
    rest = blocks[:, 16:24]
    half = LANES // 2
    rest = jnp.concatenate([rest[:, :, :half], rest[:, :, half:]], axis=1)
    size = blocks.shape[0] * 16
    return blocks[:, :16].reshape(size, LANES), rest.reshape(size, half)


def slot_order(far_bits, slots):
    at = lax.broadcasted_iota(jnp.int32, (slots, slots), 0)
    source = lax.broadcasted_iota(jnp.int32, (slots, slots), 1)
    near = at >> (far_bits + 1)
    far = (at >> 1) & ((1 << far_bits) - 1)
    return (source == far * 16 + near * 2 + (at & 1)).astype(f32).astype(bf16)


def send_kernel(place_ref, *refs):
    sources, refs = refs[:9], refs[9:]
    send_ref, mask_ref, placing_ref = refs[:3]
    targets, sems = refs[3:12], refs[12]
    copies = [
        pltpu.make_async_copy(source, target, sems.at[number])
        for number, (source, target) in enumerate(zip(sources, targets))
    ]
    for copy in copies:
        copy.start()
    slide_ref, pos_ref, owner_ref, qkv_ref, out_ref, cls_ref = targets[:6]
    bias_ref, weight_ref, features_ref = targets[6:]
    for copy in copies[:6]:
        copy.wait()
    tiles, positions, channels = features_ref.shape
    far_count = send_ref.shape[0]
    cols = weight_ref.shape[0]
    slides = owner_ref.shape[1]

    slide_row = slide_ref[...]
    owner_column = as_column(owner_ref[...].astype(f32))
    slide_ids = lax.broadcasted_iota(jnp.int32, (slides, tiles), 0)
    owners = jnp.sum(
        jnp.where(slide_ids == slide_row, owner_column, 0.0), axis=0, keepdims=True
    ).astype(jnp.int32)
    slide_values = slide_row.astype(f32)
    down = lax.broadcasted_iota(jnp.int32, (tiles, tiles), 0)
    along = lax.broadcasted_iota(jnp.int32, (tiles, tiles), 1)
    earlier = (as_column(slide_values) == slide_values) & (down < along)
    slot_rank = jnp.sum(earlier.astype(f32), axis=0, keepdims=True).astype(jnp.int32)
    owner_pair = owners >> 1
    line = sum((owner_pair >= far_count * number).astype(jnp.int32) for number in range(1, 4))
    near_owner = line * 2 + (owners & 1)
    far_owner = owner_pair - line * far_count
    target = (far_owner * 8 + near_owner) * SLOTS + slot_rank
    slots = lax.broadcasted_iota(jnp.int32, placing_ref.shape, 0)
    placing = slots == target
    tags = jnp.sum(
        jnp.where(placing, (pos_ref[...] + 1).astype(f32), 0.0), axis=1, keepdims=True
    )
    placing = placing.astype(f32).astype(bf16)
    placing_ref[...] = placing
    slot_ids = lax.broadcasted_iota(jnp.int32, (far_count * 16, LANES), 0)
    lane_ids = lax.broadcasted_iota(jnp.int32, (far_count * 16, LANES), 1)
    tag_rows = jnp.where(lane_ids == (slot_ids & 15), tags, 0.0)
    tag_rows = jnp.sum(tag_rows.reshape(far_count, 16, LANES), axis=1)

    own_rows, emb = out_ref.shape
    wc = across(out_ref[...].astype(f32), cls_ref[...], (1, 1), EXACT)
    wc_high = wc.astype(bf16).astype(f32)
    picked = []
    for part in range(3):
        block = qkv_ref[:, part * emb : part * emb + cols]
        for group in range(1, emb // cols):
            first = part * emb + group * cols
            block = jnp.where(place_ref[0] == group, qkv_ref[:, first : first + cols], block)
        picked.append(block.astype(f32))
    rows = jnp.concatenate(picked + [wc_high, wc - wc_high], axis=1)
    padded = held_rows(own_rows)
    rows = jnp.concatenate([rows, jnp.zeros((padded - own_rows, rows.shape[1]), f32)], axis=0)
    held = [rows[:, at : at + LANES] for at in range(0, rows.shape[1], LANES)]
    is_tag = lax.broadcasted_iota(jnp.int32, (padded, LANES), 0) == own_rows

    for copy in copies[6:]:
        copy.wait()
    flattened = features_ref[...].reshape(tiles * positions, channels)
    preact = across(flattened, weight_ref[...], (1, 1)) + bias_ref[...]
    mask_ref[...] = jnp.where(preact > 0, 1.0 / positions, 0.0).astype(bf16)
    summed = jnp.sum(jnp.maximum(preact, 0.0).reshape(tiles, positions, cols), axis=1)
    tile_rows = (summed * (1.0 / positions)).astype(bf16)
    blocks = fold_rows(across(placing, tile_rows, (1, 0)), far_count)
    for far in range(far_count):
        first = jnp.where(is_tag, tag_rows[far : far + 1], held[0])
        send_ref[far] = jnp.concatenate([blocks[far], first] + held[1:], axis=0).astype(bf16)


def turn_kernel(own_rows, received_ref, rows_ref, held_ref):
    far_count = received_ref.shape[0]
    slots = far_count * 16
    far_bits = far_count.bit_length() - 1
    received = received_ref[...].astype(f32)
    order = slot_order(far_bits, slots)
    wide, narrow = unfold_rows(received)
    wide = across(order, wide.astype(bf16), (1, 0))
    narrow = across(order, narrow.astype(bf16), (1, 0))
    slot = lax.broadcasted_iota(jnp.int32, (slots, far_count), 0)
    far = lax.broadcasted_iota(jnp.int32, (slots, far_count), 1)
    from_far = (((slot >> 1) & (far_count - 1)) == far).astype(f32).astype(bf16)
    tag_rows = received[:, 24 + own_rows].astype(bf16)
    slot = lax.broadcasted_iota(jnp.int32, (slots, LANES), 0)
    lane = lax.broadcasted_iota(jnp.int32, (slots, LANES), 1)
    mine = lane == (slot >> (far_bits + 1)) * 2 + (slot & 1)
    tags = jnp.sum(
        jnp.where(mine, across(from_far, tag_rows, (1, 0)), 0.0), axis=1, keepdims=True
    )
    tags = jnp.broadcast_to(tags, (slots, LANES // 2))
    rows = jnp.concatenate([wide, narrow, tags], axis=1).astype(bf16)
    rows = rows.reshape(rows_ref.shape[1:])
    for group in range(rows_ref.shape[0]):
        rows_ref[group] = rows
    padded = held_rows(own_rows)
    size = far_count * own_rows
    row = lax.broadcasted_iota(jnp.int32, (size, 1), 0).astype(f32)
    column = lax.broadcasted_iota(jnp.int32, (size, far_count * padded), 1)
    far = jnp.floor((row + 0.5) * (1.0 / own_rows))
    kept = (column == (row + far * (padded - own_rows)).astype(jnp.int32)).astype(f32).astype(bf16)
    for block in range(held_ref.shape[0] // size):
        first = 24 + block * padded
        held = received[:, first : first + padded].reshape(far_count * padded, LANES)
        held = across(kept, held.astype(bf16), (1, 0))
        held_ref[block * size : (block + 1) * size] = held.astype(bf16)


def fold_kernel(parts_ref, back_ref):
    groups, near_count, rows, cols = parts_ref.shape
    slots = near_count * rows
    total = sum(parts_ref[group].astype(f32) for group in range(groups)).reshape(slots, cols)
    far_count = back_ref.shape[0]
    order = slot_order(far_count.bit_length() - 1, slots)
    ordered = across(order, total.astype(bf16), (0, 0))
    back_ref[...] = fold_rows(ordered, far_count).astype(bf16)


def held_order(own_rows, cols):
    row = lax.broadcasted_iota(jnp.int32, (cols, cols), 0)
    place = lax.broadcasted_iota(jnp.int32, (1, cols), 1).astype(f32)
    block = jnp.floor((place + 0.5) * (1.0 / own_rows))
    far_count = cols // (2 * own_rows)
    core = (block >= far_count).astype(f32)
    source = place + (block - core * far_count + core - core * far_count) * own_rows
    return (row == source.astype(jnp.int32)).astype(f32).astype(bf16)


def weight_block(weight_ref, part, size):
    columns = []
    for block in range(weight_ref.shape[2] // size):
        pair = [weight_ref[core, part, block * size : (block + 1) * size] for core in range(2)]
        columns.append(jnp.concatenate(pair, axis=0))
    return columns


def class_block(weight_ref, order, part, size, cols):
    last = weight_ref.shape[2] // size - 1
    pair = [weight_ref[core, part, last * size :] for core in range(2)]
    both = across(order, jnp.concatenate(pair, axis=0), (1, 0))
    first = 3 * cols - last * LANES
    return both[:, first : first + CLASSES] + both[:, first + CLASSES : first + 2 * CLASSES]


def weight_grad_kernel(
    place_ref, placing_ref, back_ref, mask_ref, features_ref, kept_ref, sent_ref
):
    tiles, positions, channels = features_ref.shape
    cols = mask_ref.shape[1]
    half = cols // 2
    back = jnp.concatenate(unfold_rows(back_ref[...].astype(f32)), axis=1).astype(bf16)
    tile_grads = across(placing_ref[...], back, (0, 0))
    spread = jnp.broadcast_to(tile_grads[:, None, :], (tiles, positions, cols))
    grad_preact = spread.reshape(tiles * positions, cols) * mask_ref[...].astype(f32)
    bias = jnp.sum(grad_preact, axis=0, keepdims=True)
    flattened = features_ref[...].reshape(tiles * positions, channels)
    grad = across(grad_preact.astype(bf16), flattened, (0, 0))
    lanes = channels // kept_ref.shape[0]
    first_core = place_ref[2] == 0
    for out_ref, is_first in ((kept_ref, first_core), (sent_ref, jnp.logical_not(first_core))):
        bias_half = jnp.where(is_first, bias[:, :half], bias[:, half:])
        bias_rows = jnp.broadcast_to(
            jnp.concatenate([bias_half, jnp.zeros((1, lanes - half), f32)], axis=1), (8, lanes)
        )
        for place in range(kept_ref.shape[0]):
            block = grad[:, place * lanes : (place + 1) * lanes]
            picked = jnp.where(is_first, block[:half], block[half:])
            out_ref[place] = jnp.concatenate([picked, bias_rows], axis=0).astype(bf16)


def unpack_kernel(parts_ref, grad_ref, bias_ref):
    cores, plane, _, lanes = parts_ref.shape
    half = grad_ref.shape[0] // cores
    biases = []
    for core in range(cores):
        for place in range(plane):
            block = parts_ref[core, place].astype(f32)
            grad_ref[core * half : (core + 1) * half, place * lanes : (place + 1) * lanes] = block[
                :half
            ]
            if place == 0:
                biases.append(block[half : half + 1, :half])
    bias_ref[...] = jnp.concatenate(biases, axis=1)


def run(kernel, name, out_shape, args, specs, scratch=()):
    vmem = pl.BlockSpec(memory_space=pltpu.VMEM)
    smem = pl.BlockSpec(memory_space=pltpu.SMEM)
    kinds = {"v": vmem, "s": smem, "a": pl.BlockSpec(memory_space=pl.ANY)}
    return pl.pallas_call(
        kernel,
        out_shape=out_shape,
        in_specs=[kinds[spec] for spec in specs],
        out_specs=(vmem,) * len(out_shape),
        scratch_shapes=list(scratch),
        compiler_params=pltpu.CompilerParams(vmem_limit_bytes=(56 if scratch else 40) << 20),
        name=name,
    )(*args)


def on_device(
    features,
    tile_slide,
    tile_pos,
    slide_owner,
    slide_label,
    enc_weight,
    enc_bias,
    norm_gain,
    qkv_weight,
    out_weight,
    cls_weight,
):
    far_count = lax.axis_size(FAR)
    near_count = lax.axis_size(NEAR)
    groups = lax.axis_size("x")
    tile_count, _, channels = features.shape
    cols = enc_weight.shape[1]
    emb = cols * groups
    slot_total = far_count * near_count * SLOTS
    group_at = lax.axis_index("x")
    owner_at = lax.axis_index(ENC)

    shape = jax.ShapeDtypeStruct
    place = jnp.stack([group_at, owner_at, lax.axis_index("c")]).astype(jnp.int32)
    width = 3 * cols + 2 * CLASSES

    with jax.named_scope("encode"):
        own_rows = qkv_weight.shape[0]
        width_blocks = width // LANES
        padded = held_rows(own_rows)
        sources = (
            tile_slide.reshape(1, tile_count),
            tile_pos[None, :],
            slide_owner[None, :],
            qkv_weight,
            out_weight,
            cls_weight.T,
            enc_bias[None, :],
            enc_weight.T,
            features,
        )
        send, mask, placing = run(
            send_kernel,
            "send",
            (
                shape((far_count, 24 + width_blocks * padded, LANES), bf16),
                shape((tile_count * POS, cols), bf16),
                shape((slot_total, tile_count), bf16),
            ),
            (place,) + sources,
            "s" + "a" * len(sources),
            [pltpu.VMEM(source.shape, source.dtype) for source in sources]
            + [pltpu.SemaphoreType.DMA((len(sources),))],
        )

    with jax.named_scope("dispatch"):
        send_near, far_held = run(
            functools.partial(turn_kernel, own_rows),
            "turn",
            (
                shape((groups, near_count, far_count * SLOTS, BLOCK), bf16),
                shape((width_blocks * far_count * own_rows, LANES), bf16),
            ),
            (swap(send, FAR),),
            "v",
        )
        rows = swap(
            send_near.reshape(groups * near_count, far_count * SLOTS, BLOCK), ("x",) + NEAR
        ).reshape(groups, slot_total, BLOCK)

    with jax.named_scope("weights"):
        weights = lax.all_gather(lax.all_gather(far_held, "y", axis=0), "c", axis=0)

    with jax.named_scope("attend"):
        gain = norm_gain.reshape(groups, 1, cols)
        cls_parts = cls_weight.T.reshape(CLASSES, groups, cols).transpose(1, 0, 2)
        part_logits, att, qkv = run(
            functools.partial(forward_kernel, own_rows),
            "forward",
            (
                shape((1, CLASSES), f32),
                shape((cols // HD, slot_total, slot_total), f32),
                shape((slot_total, 3 * cols), bf16),
            ),
            (place, rows, weights, gain, cls_parts),
            "svvvv",
        )
        all_logits = lax.all_gather(part_logits, "x", axis=0)
        logits, grad_parts = run(
            functools.partial(backward_kernel, own_rows),
            "backward",
            (shape((1, CLASSES), f32), shape((groups, slot_total, cols), bf16)),
            (
                place,
                all_logits,
                slide_owner[None, :],
                slide_label[None, :],
                rows,
                weights,
                gain,
                cls_parts,
                att,
                qkv,
            ),
            "svvvvvvvvv",
        )

    with jax.named_scope("give_back"):
        from_near = swap(
            grad_parts.reshape(groups * near_count, far_count * SLOTS, cols), ("x",) + NEAR
        ).reshape(groups, near_count, far_count * SLOTS, cols)
        (folded,) = run(
            fold_kernel, "fold", (shape((far_count, 24, LANES), bf16),), (from_near,), "v"
        )
        back_rows = swap(folded, FAR)

    with jax.named_scope("encoder_grad"):
        plane_count = lax.axis_size(PLANE)
        block = (cols // 2 + 8, channels // plane_count)
        kept, sent = run(
            weight_grad_kernel,
            "weight_grad",
            (shape((plane_count,) + block, bf16),) * 2,
            (place, placing, back_rows, mask, features),
            "svvvv",
        )

    with jax.named_scope("reduce"):
        other = lax.ppermute(sent, "c", [(0, 1), (1, 0)])
        core_sum = (kept.astype(f32) + other.astype(f32)).astype(bf16)
        plane_sum = sum_blocks(core_sum, PLANE)
        total = jnp.sum(gather_copies(plane_sum, "zh").astype(f32), axis=0).astype(bf16)
        all_parts = lax.all_gather(gather_copies(total, PLANE), "c", axis=0)
        enc_grad, bias_grad = run(
            unpack_kernel,
            "unpack",
            (shape((cols, channels), f32), shape((1, cols), f32)),
            (all_parts,),
            "v",
        )
    return (logits, enc_grad.T, bias_grad[0])


def solution(mesh):
    enc_count, groups = mesh.devices.shape
    far_count = enc_count // 8
    far_lanes = 4 if far_count >= 16 else far_count // 2
    shape = (4, far_count // far_lanes, far_lanes, 2, groups)
    split = Mesh(mesh.devices.reshape(shape), ENC + ("x",))
    return jax.shard_map(
        on_device,
        mesh=split,
        in_specs=(
            P(ENC, None, None),
            P(ENC, None),
            P(ENC),
            P(),
            P(),
            P(None, "x"),
            P("x"),
            P(),
            P(ENC, None),
            P(ENC, None),
            P(),
        ),
        out_specs=(P(ENC, None), P(None, "x"), P("x")),
        check_vma=False,
    )
```

```python
import functools

import jax
import jax.numpy as jnp
from jax import lax
from jax.experimental import pallas as pl
from jax.experimental.pallas import tpu as pltpu
from jax.sharding import Mesh, PartitionSpec as P

POS = 4
HEADS = 12
CLASSES = 32
HD = 64
SLOTS = 2
BLOCK = 256
LANES = 128
FAR = ("zh", "zl")
ENC = ("y", "zh", "zl", "c")
NEAR = ("y", "c")
PLANE = ("y", "zl")
eps = 1e-05

bf16 = jnp.bfloat16
f32 = jnp.float32
EXACT = lax.Precision.HIGHEST


def across(lhs, rhs, dims, precision=None):
    return lax.dot_general(
        lhs, rhs, ((dims[:1], dims[1:]), ((), ())), precision=precision, preferred_element_type=f32
    )


def swap(blocks, axes):
    return lax.all_to_all(blocks, axes, split_axis=0, concat_axis=0, tiled=True)


def gather_copies(block, axes):
    return swap(jnp.broadcast_to(block[None], (lax.axis_size(axes),) + block.shape), axes)


def sum_blocks(blocks, axes):
    return jnp.sum(swap(blocks, axes).astype(f32), axis=0).astype(bf16)


def normed_parts(place_ref, rows_ref, cols):
    parts = [
        rows_ref[part_of(place_ref, step), :, :cols].astype(f32)
        for step in range(rows_ref.shape[0])
    ]
    width = cols * len(parts)
    mean = sum(jnp.sum(part, axis=1, keepdims=True) for part in parts) / width
    centred = [part - mean for part in parts]
    variance = sum(jnp.sum(part * part, axis=1, keepdims=True) for part in centred) / width
    inv_std = lax.rsqrt(variance + eps)
    return parts, [part * inv_std for part in centred], inv_std


def forward_kernel(
    own_rows,
    place_ref,
    rows_ref,
    weight_ref,
    gain_ref,
    cls_ref,
    logits_ref,
    att_ref,
    qkv_ref,
    weights_ref,
):
    groups, slots, _ = rows_ref.shape
    cols = gain_ref.shape[2]
    parts, normed, _ = normed_parts(place_ref, rows_ref, cols)
    size = weight_ref.shape[2] // (-(-(3 * cols + 2 * CLASSES) // LANES))
    order = held_order(own_rows, cols)
    qkv = 0.0
    for step in range(groups):
        normed_in = (normed[step] * gain_ref[part_of(place_ref, step)]).astype(bf16)
        block = across(order, weight_block(weight_ref, step, size), (1, 0)).astype(bf16)
        weights_ref[step] = block
        qkv = qkv + across(normed_in, block, (1, 0))
    qkv = qkv[:, : 3 * cols]
    column = lax.broadcasted_iota(jnp.int32, (slots, 3 * cols), 1)
    qkv = jnp.where(column < cols, qkv * HD ** (-0.5), qkv).astype(bf16)
    qkv_ref[...] = qkv
    tags = rows_ref[0, :, cols : cols + 1].astype(f32)
    count = jnp.sum(tags, axis=0, keepdims=True) * 0.0 + jnp.sum(
        (tags > 0).astype(f32), axis=0, keepdims=True
    )
    down = lax.broadcasted_iota(jnp.int32, (slots, slots), 0)
    along = lax.broadcasted_iota(jnp.int32, (slots, slots), 1)
    tag_row = jnp.sum(jnp.where(down == along, tags, 0.0), axis=0, keepdims=True)
    query_pos = tags.astype(jnp.int32) - 1
    key_pos = tag_row.astype(jnp.int32) - 1
    wc = class_block(weights_ref, place_ref, cols)
    mixed = []
    for head in range(cols // HD):
        group = head % 3
        low = (1 << group) - 1
        query_key = ((query_pos >> (6 + group)) << group) + (query_pos & low)
        key_key = ((key_pos >> (6 + group)) << group) + (key_pos & low)
        query_key = jnp.where(query_pos < 0, -1, query_key)
        key_key = jnp.where(key_pos < 0, -2, key_key)
        visible = query_key == key_key
        first = head * HD
        scores = across(
            qkv[:, first : first + HD], qkv[:, cols + first : cols + first + HD], (1, 1)
        )
        masked = jnp.where(visible, scores, -1e30)
        row_max = jnp.max(masked, axis=1, keepdims=True)
        weights = jnp.where(visible, jnp.exp(masked - row_max), 0.0)
        row_total = jnp.sum(weights, axis=1, keepdims=True)
        att = weights / jnp.where(row_total > 0, row_total, 1.0)
        att_ref[head] = att
        att_total = jnp.sum(att.astype(bf16).astype(f32), axis=0, keepdims=True)
        values = qkv[:, 2 * cols + first : 2 * cols + first + HD]
        mixed.append(across(in_terms(att_total), values, (1, 0)))
    mixed_total = jnp.sum(jnp.concatenate(mixed, axis=1), axis=0, keepdims=True)
    total = across(mixed_total, wc, (1, 0), EXACT)
    for step in range(groups):
        row_sum = jnp.sum(parts[step], axis=0, keepdims=True) * (1.0 / groups)
        total = total + across(row_sum, cls_ref[part_of(place_ref, step)], (1, 1), EXACT)
    logits_ref[...] = total / count


def backward_kernel(
    place_ref,
    part_logits_ref,
    owner_ref,
    label_ref,
    rows_ref,
    weights_ref,
    gain_ref,
    cls_ref,
    att_ref,
    qkv_ref,
    logits_ref,
    grad_ref,
):
    groups, slots, _ = rows_ref.shape
    cols = gain_ref.shape[2]
    _, normed, inv_std = normed_parts(place_ref, rows_ref, cols)
    tags = rows_ref[0, :, cols : cols + 1].astype(f32)
    live = (tags > 0).astype(f32)
    count = jnp.sum(live, axis=0, keepdims=True)
    logits = sum(part_logits_ref[part] for part in range(groups))
    logits_ref[...] = logits
    scaled = jnp.exp(logits - jnp.max(logits, axis=1, keepdims=True))
    class_probs = scaled / jnp.sum(scaled, axis=1, keepdims=True)
    mine = owner_ref[...] == place_ref[1]
    my_label = jnp.sum(jnp.where(mine, label_ref[...], 0).astype(f32), axis=1, keepdims=True)
    class_ids = lax.broadcasted_iota(jnp.int32, (1, CLASSES), 1).astype(f32)
    grad_logits = (class_probs - (class_ids == my_label).astype(f32)) / count
    wc = class_block(weights_ref, place_ref, cols)
    grad_mixed = across(grad_logits, wc, (1, 1), EXACT).astype(bf16)
    qkv = qkv_ref[...]
    grad_q, grad_k, grad_v = [], [], []
    for head in range(cols // HD):
        first = head * HD
        att = att_ref[head]
        queries = qkv[:, first : first + HD]
        keys = qkv[:, cols + first : cols + first + HD]
        values = qkv[:, 2 * cols + first : 2 * cols + first + HD]
        head_grad = grad_mixed[:, first : first + HD]
        grad_att = across(head_grad, values, (1, 1))
        expected = jnp.sum(att * grad_att, axis=1, keepdims=True)
        grad_scores = (att * (grad_att - expected)).astype(bf16)
        grad_q.append(across(grad_scores, keys, (1, 0)) * HD ** (-0.5))
        grad_k.append(across(grad_scores, queries, (0, 0)))
        spread = jnp.broadcast_to(head_grad, (slots, HD))
        grad_v.append(across(att.astype(bf16), spread, (0, 0)))
    unused = jnp.zeros((slots, 2 * CLASSES), f32)
    grad_qkv = jnp.concatenate(grad_q + grad_k + grad_v + [unused], axis=1).astype(bf16)
    scaled_parts = []
    for step in range(groups):
        grad_normed = across(grad_qkv, weights_ref[step], (1, 1))
        scaled_parts.append(grad_normed * gain_ref[part_of(place_ref, step)])
    width = cols * groups
    mean = sum(jnp.sum(e, axis=1, keepdims=True) for e in scaled_parts) / width
    slope = (
        sum(jnp.sum(e * n, axis=1, keepdims=True) for e, n in zip(scaled_parts, normed)) / width
    )
    for step in range(groups):
        part = part_of(place_ref, step)
        pooled = across(grad_logits, cls_ref[part], (1, 0), EXACT) * (1.0 / groups)
        grad = inv_std * (scaled_parts[step] - mean - normed[step] * slope)
        grad_ref[part] = fold_rows(live * pooled + grad, grad_ref.shape[1]).astype(bf16)


def as_column(row):
    size = row.shape[1]
    down = lax.broadcasted_iota(jnp.int32, (size, size), 0)
    along = lax.broadcasted_iota(jnp.int32, (size, size), 1)
    return jnp.sum(jnp.where(down == along, row, 0.0), axis=1, keepdims=True)


def in_terms(row):
    high = row.astype(bf16)
    rest = row - high.astype(f32)
    middle = rest.astype(bf16)
    low = (rest - middle.astype(f32)).astype(bf16)
    terms = [term.astype(f32) for term in (high, middle, low)]
    return jnp.concatenate(terms + [jnp.zeros((5, row.shape[1]), f32)], axis=0).astype(bf16)


def held_rows(blocks, rows):
    return (blocks * rows + 8) // 8 * 8


def fold_rows(rows, count):
    blocks = rows.reshape(count, rows.shape[0] // count, rows.shape[1])
    half = blocks.shape[1] // 2
    rest = jnp.concatenate([blocks[:, :half, LANES:], blocks[:, half:, LANES:]], axis=2)
    return jnp.concatenate([blocks[:, :, :LANES], rest], axis=1)


def unfold_rows(blocks, size):
    rest = blocks[:, size : size + size // 2]
    half = LANES // 2
    rest = jnp.concatenate([rest[:, :, :half], rest[:, :, half:]], axis=1)
    total = blocks.shape[0] * size
    return blocks[:, :size].reshape(total, LANES), rest.reshape(total, half)


def slot_order(far_bits, slots):
    at = lax.broadcasted_iota(jnp.int32, (slots, slots), 0)
    source = lax.broadcasted_iota(jnp.int32, (slots, slots), 1)
    near = at >> (far_bits + 1)
    far = (at >> 1) & ((1 << far_bits) - 1)
    return (source == far * 16 + near * 2 + (at & 1)).astype(f32).astype(bf16)


def send_kernel(place_ref, *refs):
    sources, refs = refs[:9], refs[9:]
    send_ref, mask_ref, placing_ref = refs[:3]
    targets, sems = refs[3:12], refs[12]
    copies = [
        pltpu.make_async_copy(source, target, sems.at[number])
        for number, (source, target) in enumerate(zip(sources, targets))
    ]
    for copy in copies:
        copy.start()
    slide_ref, pos_ref, owner_ref, qkv_ref, out_ref, cls_ref = targets[:6]
    bias_ref, weight_ref, features_ref = targets[6:]
    for copy in copies:
        copy.wait()
    tiles, positions, channels = features_ref.shape
    far_count = send_ref.shape[0]
    cols = weight_ref.shape[0]
    slides = owner_ref.shape[1]

    slide_row = slide_ref[...]
    owner_column = as_column(owner_ref[...].astype(f32))
    slide_ids = lax.broadcasted_iota(jnp.int32, (slides, tiles), 0)
    owners = jnp.sum(
        jnp.where(slide_ids == slide_row, owner_column, 0.0), axis=0, keepdims=True
    ).astype(jnp.int32)
    slide_values = slide_row.astype(f32)
    down = lax.broadcasted_iota(jnp.int32, (tiles, tiles), 0)
    along = lax.broadcasted_iota(jnp.int32, (tiles, tiles), 1)
    earlier = (as_column(slide_values) == slide_values) & (down < along)
    slot_rank = jnp.sum(earlier.astype(f32), axis=0, keepdims=True).astype(jnp.int32)
    owner_pair = owners >> 1
    line = sum((owner_pair >= far_count * number).astype(jnp.int32) for number in range(1, 4))
    near_owner = line * 2 + (owners & 1)
    far_owner = owner_pair - line * far_count
    target = (far_owner * 8 + near_owner) * SLOTS + slot_rank
    slots = lax.broadcasted_iota(jnp.int32, placing_ref.shape, 0)
    placing = slots == target
    tags = jnp.sum(
        jnp.where(placing, (pos_ref[...] + 1).astype(f32), 0.0), axis=1, keepdims=True
    )
    placing = placing.astype(f32).astype(bf16)
    placing_ref[...] = placing
    slot_ids = lax.broadcasted_iota(jnp.int32, (far_count * 16, LANES), 0)
    lane_ids = lax.broadcasted_iota(jnp.int32, (far_count * 16, LANES), 1)
    tag_rows = jnp.where(lane_ids == (slot_ids & 15), tags, 0.0)
    tag_rows = jnp.sum(tag_rows.reshape(far_count, 16, LANES), axis=1)

    own_rows, emb = out_ref.shape
    wc = across(out_ref[...].astype(f32), cls_ref[...], (1, 1), EXACT)
    wc_high = wc.astype(bf16).astype(f32)
    picked = []
    for part in range(3):
        block = qkv_ref[:, part * emb : part * emb + cols]
        for group in range(1, emb // cols):
            first = part * emb + group * cols
            block = jnp.where(place_ref[0] == group, qkv_ref[:, first : first + cols], block)
        picked.append(block.astype(f32))
    rows = jnp.concatenate(picked + [wc_high, wc - wc_high], axis=1)
    held = [rows[:, at : at + LANES] for at in range(0, rows.shape[1], LANES)]
    tag_at = len(held) * own_rows
    padded = held_rows(len(held), own_rows)
    held = jnp.concatenate(held + [jnp.zeros((padded - tag_at, LANES), f32)], axis=0)
    is_tag = lax.broadcasted_iota(jnp.int32, (padded, LANES), 0) == tag_at
    flattened = features_ref[...].reshape(tiles * positions, channels)
    preact = across(flattened, weight_ref[...], (1, 1)) + bias_ref[...]
    mask_ref[...] = jnp.where(preact > 0, 1.0 / positions, 0.0).astype(bf16)
    summed = jnp.sum(jnp.maximum(preact, 0.0).reshape(tiles, positions, cols), axis=1)
    tile_rows = (summed * (1.0 / positions)).astype(bf16)
    blocks = fold_rows(across(placing, tile_rows, (1, 0)), far_count)
    for far in range(far_count):
        rest = jnp.where(is_tag, tag_rows[far : far + 1], held)
        send_ref[far] = jnp.concatenate([blocks[far], rest], axis=0).astype(bf16)


def turn_kernel(own_rows, received_ref, rows_ref, held_ref):
    far_count = received_ref.shape[0]
    slots = far_count * 16
    far_bits = far_count.bit_length() - 1
    received = received_ref[...].astype(f32)
    order = slot_order(far_bits, slots)
    wide, narrow = unfold_rows(received, 16)
    wide = across(order, wide.astype(bf16), (1, 0))
    narrow = across(order, narrow.astype(bf16), (1, 0))
    slot = lax.broadcasted_iota(jnp.int32, (slots, far_count), 0)
    far = lax.broadcasted_iota(jnp.int32, (slots, far_count), 1)
    from_far = (((slot >> 1) & (far_count - 1)) == far).astype(f32).astype(bf16)
    size = far_count * own_rows
    block_count = held_ref.shape[0] // size
    tag_rows = received[:, 24 + block_count * own_rows].astype(bf16)
    slot = lax.broadcasted_iota(jnp.int32, (slots, LANES), 0)
    lane = lax.broadcasted_iota(jnp.int32, (slots, LANES), 1)
    mine = lane == (slot >> (far_bits + 1)) * 2 + (slot & 1)
    tags = jnp.sum(
        jnp.where(mine, across(from_far, tag_rows, (1, 0)), 0.0), axis=1, keepdims=True
    )
    tags = jnp.broadcast_to(tags, (slots, LANES // 2))
    rows = jnp.concatenate([wide, narrow, tags], axis=1).astype(bf16)
    rows = rows.reshape(rows_ref.shape[1:])
    for group in range(rows_ref.shape[0]):
        rows_ref[group] = rows
    padded = received.shape[1] - 24
    held = received[:, 24:].reshape(far_count * padded, LANES).astype(bf16)
    row = lax.broadcasted_iota(jnp.int32, (size, 1), 0).astype(f32)
    column = lax.broadcasted_iota(jnp.int32, (size, far_count * padded), 1)
    far = jnp.floor((row + 0.5) * (1.0 / own_rows))
    source = (row + far * (padded - own_rows)).astype(jnp.int32)
    for block in range(block_count):
        kept = (column == source + block * own_rows).astype(f32).astype(bf16)
        held_ref[block * size : (block + 1) * size] = across(kept, held, (1, 0)).astype(bf16)


def fold_kernel(parts_ref, back_ref):
    groups = parts_ref.shape[0]
    far_count = back_ref.shape[0]
    total = sum(parts_ref[group].astype(f32) for group in range(groups))
    wide, narrow = unfold_rows(total, far_count * SLOTS)
    total = jnp.concatenate([wide, narrow], axis=1).astype(bf16)
    order = slot_order(far_count.bit_length() - 1, total.shape[0])
    back_ref[...] = fold_rows(across(order, total, (0, 0)), far_count).astype(bf16)


def held_order(own_rows, cols):
    row = lax.broadcasted_iota(jnp.int32, (cols, cols), 0)
    place = lax.broadcasted_iota(jnp.int32, (1, cols), 1).astype(f32)
    block = jnp.floor((place + 0.5) * (1.0 / own_rows))
    far_count = cols // (2 * own_rows)
    core = (block >= far_count).astype(f32)
    source = place + (block - core * far_count + core - core * far_count) * own_rows
    return (row == source.astype(jnp.int32)).astype(f32).astype(bf16)


def weight_block(weight_ref, step, size):
    columns = []
    for block in range(weight_ref.shape[2] // size):
        pair = [weight_ref[core, step, block * size : (block + 1) * size] for core in range(2)]
        columns.append(jnp.concatenate(pair, axis=0))
    return jnp.concatenate(columns, axis=1)


def part_of(place_ref, step):
    return place_ref[3] ^ step


def class_block(weights_ref, place_ref, cols):
    mine = weights_ref[place_ref[3] ^ place_ref[0]]
    both = mine[:, 3 * cols :].astype(f32)
    return both[:, :CLASSES] + both[:, CLASSES : 2 * CLASSES]


def weight_grad_kernel(
    place_ref, placing_ref, back_ref, mask_ref, features_ref, kept_ref, sent_ref
):
    tiles, positions, channels = features_ref.shape
    cols = mask_ref.shape[1]
    half = cols // 2
    back = jnp.concatenate(unfold_rows(back_ref[...].astype(f32), 16), axis=1).astype(bf16)
    tile_grads = across(placing_ref[...], back, (0, 0))
    spread = jnp.broadcast_to(tile_grads[:, None, :], (tiles, positions, cols))
    grad_preact = spread.reshape(tiles * positions, cols) * mask_ref[...].astype(f32)
    bias = jnp.sum(grad_preact, axis=0, keepdims=True)
    flattened = features_ref[...].reshape(tiles * positions, channels)
    grad = across(grad_preact.astype(bf16), flattened, (0, 0))
    lanes = channels // kept_ref.shape[0]
    first_core = place_ref[2] == 0
    for out_ref, is_first in ((kept_ref, first_core), (sent_ref, jnp.logical_not(first_core))):
        bias_half = jnp.where(is_first, bias[:, :half], bias[:, half:])
        bias_rows = jnp.broadcast_to(
            jnp.concatenate([bias_half, jnp.zeros((1, lanes - half), f32)], axis=1), (8, lanes)
        )
        for place in range(kept_ref.shape[0]):
            block = grad[:, place * lanes : (place + 1) * lanes]
            picked = jnp.where(is_first, block[:half], block[half:])
            out_ref[place] = jnp.concatenate([picked, bias_rows], axis=0).astype(bf16)


def unpack_kernel(parts_ref, grad_ref, bias_ref):
    cores, plane, _, lanes = parts_ref.shape
    half = grad_ref.shape[0] // cores
    biases = []
    for core in range(cores):
        for place in range(plane):
            block = parts_ref[core, place].astype(f32)
            grad_ref[core * half : (core + 1) * half, place * lanes : (place + 1) * lanes] = block[
                :half
            ]
            if place == 0:
                biases.append(block[half : half + 1, :half])
    bias_ref[...] = jnp.concatenate(biases, axis=1)


def run(kernel, name, out_shape, args, specs, scratch=()):
    vmem = pl.BlockSpec(memory_space=pltpu.VMEM)
    smem = pl.BlockSpec(memory_space=pltpu.SMEM)
    kinds = {"v": vmem, "s": smem, "a": pl.BlockSpec(memory_space=pl.ANY)}
    return pl.pallas_call(
        kernel,
        out_shape=out_shape,
        in_specs=[kinds[spec] for spec in specs],
        out_specs=(vmem,) * len(out_shape),
        scratch_shapes=list(scratch),
        compiler_params=pltpu.CompilerParams(vmem_limit_bytes=(56 if scratch else 40) << 20),
        name=name,
    )(*args)


def on_device(
    features,
    tile_slide,
    tile_pos,
    slide_owner,
    slide_label,
    enc_weight,
    enc_bias,
    norm_gain,
    qkv_weight,
    out_weight,
    cls_weight,
):
    far_count = lax.axis_size(FAR)
    near_count = lax.axis_size(NEAR)
    groups = lax.axis_size("x")
    tile_count, _, channels = features.shape
    cols = enc_weight.shape[1]
    emb = cols * groups
    slot_total = far_count * near_count * SLOTS
    group_at = lax.axis_index("x")
    owner_at = lax.axis_index(ENC)

    shape = jax.ShapeDtypeStruct
    place = jnp.stack([group_at, owner_at, lax.axis_index("c"), lax.axis_index("y")]).astype(
        jnp.int32
    )
    width = 3 * cols + 2 * CLASSES

    with jax.named_scope("encode"):
        own_rows = qkv_weight.shape[0]
        width_blocks = width // LANES
        sources = (
            tile_slide.reshape(1, tile_count),
            tile_pos[None, :],
            slide_owner[None, :],
            qkv_weight,
            out_weight,
            cls_weight.T,
            enc_bias[None, :],
            enc_weight.T,
            features,
        )
        send, mask, placing = run(
            send_kernel,
            "send",
            (
                shape((far_count, 24 + held_rows(width_blocks, own_rows), LANES), bf16),
                shape((tile_count * POS, cols), bf16),
                shape((slot_total, tile_count), bf16),
            ),
            (place,) + sources,
            "s" + "a" * len(sources),
            [pltpu.VMEM(source.shape, source.dtype) for source in sources]
            + [pltpu.SemaphoreType.DMA((len(sources),))],
        )

    with jax.named_scope("dispatch"):
        send_near, far_held = run(
            functools.partial(turn_kernel, own_rows),
            "turn",
            (
                shape((groups, near_count, far_count * SLOTS, BLOCK), bf16),
                shape((width_blocks * far_count * own_rows, LANES), bf16),
            ),
            (swap(send, FAR),),
            "v",
        )
        rows = swap(
            send_near.reshape(groups * near_count, far_count * SLOTS, BLOCK), ("x",) + NEAR
        ).reshape(groups, slot_total, BLOCK)

    with jax.named_scope("weights"):
        steps = [
            lax.ppermute(far_held, "y", [(at, at ^ step) for at in range(4)]) for step in range(1, 4)
        ]
        weights = lax.all_gather(jnp.stack([far_held] + steps), "c", axis=0)

    with jax.named_scope("attend"):
        gain = norm_gain.reshape(groups, 1, cols)
        cls_parts = cls_weight.T.reshape(CLASSES, groups, cols).transpose(1, 0, 2)
        part_logits, att, qkv, ordered = run(
            functools.partial(forward_kernel, own_rows),
            "forward",
            (
                shape((1, CLASSES), f32),
                shape((cols // HD, slot_total, slot_total), f32),
                shape((slot_total, 3 * cols), bf16),
                shape((groups, cols, width), bf16),
            ),
            (place, rows, weights, gain, cls_parts),
            "svvvv",
        )
        all_logits = lax.all_gather(part_logits, "x", axis=0)
        logits, grad_parts = run(
            backward_kernel,
            "backward",
            (
                shape((1, CLASSES), f32),
                shape((groups, near_count, far_count * SLOTS * 3 // 2, LANES), bf16),
            ),
            (
                place,
                all_logits,
                slide_owner[None, :],
                slide_label[None, :],
                rows,
                ordered,
                gain,
                cls_parts,
                att,
                qkv,
            ),
            "svvvvvvvvv",
        )

    with jax.named_scope("give_back"):
        from_near = swap(
            grad_parts.reshape((groups * near_count,) + grad_parts.shape[2:]), ("x",) + NEAR
        ).reshape(grad_parts.shape)
        (folded,) = run(
            fold_kernel, "fold", (shape((far_count, 24, LANES), bf16),), (from_near,), "v"
        )
        back_rows = swap(folded, FAR)

    with jax.named_scope("encoder_grad"):
        plane_count = lax.axis_size(PLANE)
        block = (cols // 2 + 8, channels // plane_count)
        kept, sent = run(
            weight_grad_kernel,
            "weight_grad",
            (shape((plane_count,) + block, bf16),) * 2,
            (place, placing, back_rows, mask, features),
            "svvvv",
        )

    with jax.named_scope("reduce"):
        other = lax.ppermute(sent, "c", [(0, 1), (1, 0)])
        core_sum = (kept.astype(f32) + other.astype(f32)).astype(bf16)
        plane_sum = sum_blocks(core_sum, PLANE)
        total = jnp.sum(gather_copies(plane_sum, "zh").astype(f32), axis=0).astype(bf16)
        all_parts = lax.all_gather(gather_copies(total, PLANE), "c", axis=0)
        enc_grad, bias_grad = run(
            unpack_kernel,
            "unpack",
            (shape((cols, channels), f32), shape((1, cols), f32)),
            (all_parts,),
            "v",
        )
    return (logits, enc_grad.T, bias_grad[0])


def solution(mesh):
    enc_count, groups = mesh.devices.shape
    far_count = enc_count // 8
    far_lanes = 4 if far_count >= 16 else far_count // 2
    shape = (4, far_count // far_lanes, far_lanes, 2, groups)
    split = Mesh(mesh.devices.reshape(shape), ENC + ("x",))
    return jax.shard_map(
        on_device,
        mesh=split,
        in_specs=(
            P(ENC, None, None),
            P(ENC, None),
            P(ENC),
            P(),
            P(),
            P(None, "x"),
            P("x"),
            P(),
            P(ENC, None),
            P(ENC, None),
            P(),
        ),
        out_specs=(P(ENC, None), P(None, "x"), P("x")),
        check_vma=False,
    )
```

```python
import functools

import jax
import jax.numpy as jnp
from jax import lax
from jax.experimental import pallas as pl
from jax.experimental.pallas import tpu as pltpu
from jax.sharding import Mesh, PartitionSpec as P

POS = 4
HEADS = 12
CLASSES = 32
HD = 64
SLOTS = 2
BLOCK = 256
LANES = 128
FAR = ("zh", "zl")
ENC = ("y", "zh", "zl", "c")
NEAR = ("y", "c")
PLANE = ("y", "zl")
eps = 1e-05

bf16 = jnp.bfloat16
f32 = jnp.float32
EXACT = lax.Precision.HIGHEST


def across(lhs, rhs, dims, precision=None):
    return lax.dot_general(
        lhs, rhs, ((dims[:1], dims[1:]), ((), ())), precision=precision, preferred_element_type=f32
    )


def swap(blocks, axes):
    return lax.all_to_all(blocks, axes, split_axis=0, concat_axis=0, tiled=True)


def plane_groups():
    lines, far_count, cores = 4, lax.axis_size(FAR), 2
    length = lax.axis_size("zl")
    groups = []
    for core in range(cores):
        for first in range(0, far_count, length):
            stretch = [(first + core * length // 2 + at) % far_count for at in range(length)]
            groups.append(
                [(line * far_count + far) * cores + core for line in range(lines) for far in stretch]
            )
    return groups


def swap_plane(blocks):
    return lax.all_to_all(
        blocks, ENC, split_axis=0, concat_axis=0, axis_index_groups=plane_groups(), tiled=True
    )


def gather_copies(block, axes):
    return swap(jnp.broadcast_to(block[None], (lax.axis_size(axes),) + block.shape), axes)


def sum_blocks(blocks, axes):
    return jnp.sum(swap(blocks, axes).astype(f32), axis=0).astype(bf16)


def normed_parts(rows_ref, cols):
    parts = [
        rows_ref[part, :, :cols].astype(f32)
        for part in range(rows_ref.shape[0])
    ]
    width = cols * len(parts)
    mean = sum(jnp.sum(part, axis=1, keepdims=True) for part in parts) / width
    centred = [part - mean for part in parts]
    variance = sum(jnp.sum(part * part, axis=1, keepdims=True) for part in centred) / width
    inv_std = lax.rsqrt(variance + eps)
    return parts, [part * inv_std for part in centred], inv_std


def forward_kernel(
    own_rows,
    place_ref,
    rows_ref,
    weight_ref,
    gain_ref,
    cls_ref,
    logits_ref,
    att_ref,
    qkv_ref,
    weights_ref,
):
    groups, slots, _ = rows_ref.shape
    cols = gain_ref.shape[2]
    parts, normed, _ = normed_parts(rows_ref, cols)
    size = weight_ref.shape[1] // (-(-(3 * cols + 2 * CLASSES) // LANES))
    order = held_order(own_rows, cols)
    qkv = 0.0
    for part in range(groups):
        normed_in = (normed[part] * gain_ref[part]).astype(bf16)
        block = across(order, weight_block(weight_ref, part, size), (1, 0)).astype(bf16)
        weights_ref[part] = block
        qkv = qkv + across(normed_in, block, (1, 0))
    qkv = qkv[:, : 3 * cols]
    column = lax.broadcasted_iota(jnp.int32, (slots, 3 * cols), 1)
    qkv = jnp.where(column < cols, qkv * HD ** (-0.5), qkv).astype(bf16)
    qkv_ref[...] = qkv
    tags = rows_ref[0, :, cols : cols + 1].astype(f32)
    count = jnp.sum(tags, axis=0, keepdims=True) * 0.0 + jnp.sum(
        (tags > 0).astype(f32), axis=0, keepdims=True
    )
    down = lax.broadcasted_iota(jnp.int32, (slots, slots), 0)
    along = lax.broadcasted_iota(jnp.int32, (slots, slots), 1)
    tag_row = jnp.sum(jnp.where(down == along, tags, 0.0), axis=0, keepdims=True)
    query_pos = tags.astype(jnp.int32) - 1
    key_pos = tag_row.astype(jnp.int32) - 1
    wc = class_block(weights_ref, place_ref, cols)
    mixed = []
    for head in range(cols // HD):
        group = head % 3
        low = (1 << group) - 1
        query_key = ((query_pos >> (6 + group)) << group) + (query_pos & low)
        key_key = ((key_pos >> (6 + group)) << group) + (key_pos & low)
        query_key = jnp.where(query_pos < 0, -1, query_key)
        key_key = jnp.where(key_pos < 0, -2, key_key)
        visible = query_key == key_key
        first = head * HD
        scores = across(
            qkv[:, first : first + HD], qkv[:, cols + first : cols + first + HD], (1, 1)
        )
        masked = jnp.where(visible, scores, -1e30)
        row_max = jnp.max(masked, axis=1, keepdims=True)
        weights = jnp.where(visible, jnp.exp(masked - row_max), 0.0)
        row_total = jnp.sum(weights, axis=1, keepdims=True)
        att = weights / jnp.where(row_total > 0, row_total, 1.0)
        att_ref[head] = att
        att_total = jnp.sum(att.astype(bf16).astype(f32), axis=0, keepdims=True)
        values = qkv[:, 2 * cols + first : 2 * cols + first + HD]
        mixed.append(across(in_terms(att_total), values, (1, 0)))
    mixed_total = jnp.sum(jnp.concatenate(mixed, axis=1), axis=0, keepdims=True)
    total = fine(mixed_total, wc, (1, 0))
    for part in range(groups):
        row_sum = jnp.sum(parts[part], axis=0, keepdims=True) * (1.0 / groups)
        total = total + fine(row_sum, cls_ref[part], (1, 1))
    logits_ref[...] = total / count


def backward_kernel(
    place_ref,
    part_logits_ref,
    owner_ref,
    label_ref,
    rows_ref,
    weights_ref,
    gain_ref,
    cls_ref,
    att_ref,
    qkv_ref,
    logits_ref,
    grad_ref,
):
    groups, slots, _ = rows_ref.shape
    cols = gain_ref.shape[2]
    _, normed, inv_std = normed_parts(rows_ref, cols)
    tags = rows_ref[0, :, cols : cols + 1].astype(f32)
    live = (tags > 0).astype(f32)
    count = jnp.sum(live, axis=0, keepdims=True)
    logits = sum(part_logits_ref[part] for part in range(groups))
    logits_ref[...] = logits
    scaled = jnp.exp(logits - jnp.max(logits, axis=1, keepdims=True))
    class_probs = scaled / jnp.sum(scaled, axis=1, keepdims=True)
    mine = owner_ref[...] == place_ref[1]
    my_label = jnp.sum(jnp.where(mine, label_ref[...], 0).astype(f32), axis=1, keepdims=True)
    class_ids = lax.broadcasted_iota(jnp.int32, (1, CLASSES), 1).astype(f32)
    grad_logits = (class_probs - (class_ids == my_label).astype(f32)) / count
    wc = class_block(weights_ref, place_ref, cols)
    grad_mixed = fine(grad_logits, wc, (1, 1)).astype(bf16)
    qkv = qkv_ref[...]
    grad_q, grad_k, grad_v = [], [], []
    for head in range(cols // HD):
        first = head * HD
        att = att_ref[head]
        queries = qkv[:, first : first + HD]
        keys = qkv[:, cols + first : cols + first + HD]
        values = qkv[:, 2 * cols + first : 2 * cols + first + HD]
        head_grad = grad_mixed[:, first : first + HD]
        grad_att = across(head_grad, values, (1, 1))
        expected = jnp.sum(att * grad_att, axis=1, keepdims=True)
        grad_scores = (att * (grad_att - expected)).astype(bf16)
        grad_q.append(across(grad_scores, keys, (1, 0)) * HD ** (-0.5))
        grad_k.append(across(grad_scores, queries, (0, 0)))
        spread = jnp.broadcast_to(head_grad, (slots, HD))
        grad_v.append(across(att.astype(bf16), spread, (0, 0)))
    unused = jnp.zeros((slots, 2 * CLASSES), f32)
    grad_qkv = jnp.concatenate(grad_q + grad_k + grad_v + [unused], axis=1).astype(bf16)
    scaled_parts = []
    for part in range(groups):
        grad_normed = across(grad_qkv, weights_ref[part], (1, 1))
        scaled_parts.append(grad_normed * gain_ref[part])
    width = cols * groups
    mean = sum(jnp.sum(e, axis=1, keepdims=True) for e in scaled_parts) / width
    slope = (
        sum(jnp.sum(e * n, axis=1, keepdims=True) for e, n in zip(scaled_parts, normed)) / width
    )
    for part in range(groups):
        pooled = fine(grad_logits, cls_ref[part], (1, 0)) * (1.0 / groups)
        grad = inv_std * (scaled_parts[part] - mean - normed[part] * slope)
        grad_ref[part] = fold_rows(live * pooled + grad, grad_ref.shape[1]).astype(bf16)


def as_column(row):
    size = row.shape[1]
    down = lax.broadcasted_iota(jnp.int32, (size, size), 0)
    along = lax.broadcasted_iota(jnp.int32, (size, size), 1)
    return jnp.sum(jnp.where(down == along, row, 0.0), axis=1, keepdims=True)


def in_terms(row):
    high = row.astype(bf16)
    rest = row - high.astype(f32)
    middle = rest.astype(bf16)
    low = (rest - middle.astype(f32)).astype(bf16)
    terms = [term.astype(f32) for term in (high, middle, low)]
    return jnp.concatenate(terms + [jnp.zeros((5, row.shape[1]), f32)], axis=0).astype(bf16)


def fine(row, matrix, dims):
    terms = in_terms(row)
    high = matrix.astype(bf16)
    low = (matrix - high.astype(f32)).astype(bf16)
    summed = across(terms, high, dims) + across(terms, low, dims)
    return jnp.sum(summed, axis=0, keepdims=True)


def held_rows(blocks, rows):
    return (blocks * rows + 8) // 8 * 8


def fold_rows(rows, count):
    blocks = rows.reshape(count, rows.shape[0] // count, rows.shape[1])
    half = blocks.shape[1] // 2
    rest = jnp.concatenate([blocks[:, :half, LANES:], blocks[:, half:, LANES:]], axis=2)
    return jnp.concatenate([blocks[:, :, :LANES], rest], axis=1)


def unfold_rows(blocks, size):
    rest = blocks[:, size : size + size // 2]
    half = LANES // 2
    rest = jnp.concatenate([rest[:, :, :half], rest[:, :, half:]], axis=1)
    total = blocks.shape[0] * size
    return blocks[:, :size].reshape(total, LANES), rest.reshape(total, half)


def slot_order(far_bits, slots):
    at = lax.broadcasted_iota(jnp.int32, (slots, slots), 0)
    source = lax.broadcasted_iota(jnp.int32, (slots, slots), 1)
    near = at >> (far_bits + 1)
    far = (at >> 1) & ((1 << far_bits) - 1)
    return (source == far * 16 + near * 2 + (at & 1)).astype(f32).astype(bf16)


def send_kernel(place_ref, *refs):
    sources, refs = refs[:9], refs[9:]
    send_ref, mask_ref, placing_ref = refs[:3]
    targets, sems = refs[3:12], refs[12]
    copies = [
        pltpu.make_async_copy(source, target, sems.at[number])
        for number, (source, target) in enumerate(zip(sources, targets))
    ]
    for copy in copies:
        copy.start()
    slide_ref, pos_ref, owner_ref, qkv_ref, out_ref, cls_ref = targets[:6]
    bias_ref, weight_ref, features_ref = targets[6:]
    for copy in copies:
        copy.wait()
    tiles, positions, channels = features_ref.shape
    far_count = send_ref.shape[0]
    cols = weight_ref.shape[0]
    slides = owner_ref.shape[1]

    slide_row = slide_ref[...]
    owner_column = as_column(owner_ref[...].astype(f32))
    slide_ids = lax.broadcasted_iota(jnp.int32, (slides, tiles), 0)
    owners = jnp.sum(
        jnp.where(slide_ids == slide_row, owner_column, 0.0), axis=0, keepdims=True
    ).astype(jnp.int32)
    slide_values = slide_row.astype(f32)
    down = lax.broadcasted_iota(jnp.int32, (tiles, tiles), 0)
    along = lax.broadcasted_iota(jnp.int32, (tiles, tiles), 1)
    earlier = (as_column(slide_values) == slide_values) & (down < along)
    slot_rank = jnp.sum(earlier.astype(f32), axis=0, keepdims=True).astype(jnp.int32)
    owner_pair = owners >> 1
    line = sum((owner_pair >= far_count * number).astype(jnp.int32) for number in range(1, 4))
    near_owner = line * 2 + (owners & 1)
    far_owner = owner_pair - line * far_count
    target = (far_owner * 8 + near_owner) * SLOTS + slot_rank
    slots = lax.broadcasted_iota(jnp.int32, placing_ref.shape, 0)
    placing = slots == target
    tags = jnp.sum(
        jnp.where(placing, (pos_ref[...] + 1).astype(f32), 0.0), axis=1, keepdims=True
    )
    placing = placing.astype(f32).astype(bf16)
    placing_ref[...] = placing
    slot_ids = lax.broadcasted_iota(jnp.int32, (far_count * 16, LANES), 0)
    lane_ids = lax.broadcasted_iota(jnp.int32, (far_count * 16, LANES), 1)
    tag_rows = jnp.where(lane_ids == (slot_ids & 15), tags, 0.0)
    tag_rows = jnp.sum(tag_rows.reshape(far_count, 16, LANES), axis=1)

    own_rows, emb = out_ref.shape
    wc = across(out_ref[...].astype(f32), cls_ref[...], (1, 1), EXACT)
    wc_high = wc.astype(bf16).astype(f32)
    picked = []
    for part in range(3):
        block = qkv_ref[:, part * emb : part * emb + cols]
        for group in range(1, emb // cols):
            first = part * emb + group * cols
            block = jnp.where(place_ref[0] == group, qkv_ref[:, first : first + cols], block)
        picked.append(block.astype(f32))
    rows = jnp.concatenate(picked + [wc_high, wc - wc_high], axis=1)
    held = [rows[:, at : at + LANES] for at in range(0, rows.shape[1], LANES)]
    tag_at = len(held) * own_rows
    padded = held_rows(len(held), own_rows)
    held = jnp.concatenate(held + [jnp.zeros((padded - tag_at, LANES), f32)], axis=0)
    is_tag = lax.broadcasted_iota(jnp.int32, (padded, LANES), 0) == tag_at
    flattened = features_ref[...].reshape(tiles * positions, channels)
    preact = across(flattened, weight_ref[...], (1, 1)) + bias_ref[...]
    mask_ref[...] = jnp.where(preact > 0, 1.0 / positions, 0.0).astype(bf16)
    summed = jnp.sum(jnp.maximum(preact, 0.0).reshape(tiles, positions, cols), axis=1)
    tile_rows = (summed * (1.0 / positions)).astype(bf16)
    blocks = fold_rows(across(placing, tile_rows, (1, 0)), far_count)
    for far in range(far_count):
        rest = jnp.where(is_tag, tag_rows[far : far + 1], held)
        send_ref[far] = jnp.concatenate([blocks[far], rest], axis=0).astype(bf16)


def turn_kernel(own_rows, received_ref, rows_ref, held_ref):
    far_count = received_ref.shape[0]
    slots = far_count * 16
    far_bits = far_count.bit_length() - 1
    received = received_ref[...].astype(f32)
    order = slot_order(far_bits, slots)
    wide, narrow = unfold_rows(received, 16)
    wide = across(order, wide.astype(bf16), (1, 0))
    narrow = across(order, narrow.astype(bf16), (1, 0))
    slot = lax.broadcasted_iota(jnp.int32, (slots, far_count), 0)
    far = lax.broadcasted_iota(jnp.int32, (slots, far_count), 1)
    from_far = (((slot >> 1) & (far_count - 1)) == far).astype(f32).astype(bf16)
    size = far_count * own_rows
    block_count = held_ref.shape[0] // size
    tag_rows = received[:, 24 + block_count * own_rows].astype(bf16)
    slot = lax.broadcasted_iota(jnp.int32, (slots, LANES), 0)
    lane = lax.broadcasted_iota(jnp.int32, (slots, LANES), 1)
    mine = lane == (slot >> (far_bits + 1)) * 2 + (slot & 1)
    tags = jnp.sum(
        jnp.where(mine, across(from_far, tag_rows, (1, 0)), 0.0), axis=1, keepdims=True
    )
    tags = jnp.broadcast_to(tags, (slots, LANES // 2))
    rows = jnp.concatenate([wide, narrow, tags], axis=1).astype(bf16)
    rows = rows.reshape(rows_ref.shape[1:])
    for group in range(rows_ref.shape[0]):
        rows_ref[group] = rows
    padded = received.shape[1] - 24
    held = received[:, 24:].reshape(far_count * padded, LANES).astype(bf16)
    row = lax.broadcasted_iota(jnp.int32, (size, 1), 0).astype(f32)
    column = lax.broadcasted_iota(jnp.int32, (size, far_count * padded), 1)
    far = jnp.floor((row + 0.5) * (1.0 / own_rows))
    source = (row + far * (padded - own_rows)).astype(jnp.int32)
    for block in range(block_count):
        kept = (column == source + block * own_rows).astype(f32).astype(bf16)
        held_ref[block * size : (block + 1) * size] = across(kept, held, (1, 0)).astype(bf16)


def fold_kernel(parts_ref, back_ref):
    groups = parts_ref.shape[0]
    far_count = back_ref.shape[0]
    total = sum(parts_ref[group].astype(f32) for group in range(groups))
    wide, narrow = unfold_rows(total, far_count * SLOTS)
    total = jnp.concatenate([wide, narrow], axis=1).astype(bf16)
    order = slot_order(far_count.bit_length() - 1, total.shape[0])
    back_ref[...] = fold_rows(across(order, total, (0, 0)), far_count).astype(bf16)


def held_order(own_rows, cols):
    row = lax.broadcasted_iota(jnp.int32, (cols, cols), 0)
    place = lax.broadcasted_iota(jnp.int32, (1, cols), 1).astype(f32)
    block = jnp.floor((place + 0.5) * (1.0 / own_rows))
    far_count = cols // (2 * own_rows)
    core = (block >= far_count).astype(f32)
    source = place + (block - core * far_count + core - core * far_count) * own_rows
    return (row == source.astype(jnp.int32)).astype(f32).astype(bf16)


def weight_block(weight_ref, part, size):
    columns = []
    for block in range(weight_ref.shape[1] // size):
        pair = [
            weight_ref[part * 2 + core, block * size : (block + 1) * size] for core in range(2)
        ]
        columns.append(jnp.concatenate(pair, axis=0))
    return jnp.concatenate(columns, axis=1)


def class_block(weights_ref, place_ref, cols):
    mine = weights_ref[place_ref[0]]
    both = mine[:, 3 * cols :].astype(f32)
    return both[:, :CLASSES] + both[:, CLASSES : 2 * CLASSES]


def weight_grad_kernel(
    of_other, place_ref, placing_ref, back_ref, mask_ref, features_ref, half_ref
):
    tiles, positions, channels = features_ref.shape
    half = mask_ref.shape[1] // 2
    is_first = place_ref[2] == (1 if of_other else 0)
    back = jnp.concatenate(unfold_rows(back_ref[...].astype(f32), 16), axis=1)
    back = jnp.where(is_first, back[:, :half], back[:, half:]).astype(bf16)
    mask = mask_ref[...].astype(f32)
    mask = jnp.where(is_first, mask[:, :half], mask[:, half:])
    tile_grads = across(placing_ref[...], back, (0, 0))
    spread = jnp.broadcast_to(tile_grads[:, None, :], (tiles, positions, half))
    grad_preact = spread.reshape(tiles * positions, half) * mask
    bias = jnp.sum(grad_preact, axis=0, keepdims=True)
    flattened = features_ref[...].reshape(tiles * positions, channels)
    grad = across(grad_preact.astype(bf16), flattened, (0, 0))
    lanes = channels // half_ref.shape[0]
    bias_rows = jnp.concatenate([bias, jnp.zeros((1, lanes - half), f32)], axis=1)
    bias_rows = jnp.broadcast_to(bias_rows, (8, lanes))
    for place in range(half_ref.shape[0]):
        block = grad[:, place * lanes : (place + 1) * lanes]
        half_ref[place] = jnp.concatenate([block, bias_rows], axis=0).astype(bf16)


def unpack_kernel(parts_ref, grad_ref, bias_ref):
    cores, plane, _, lanes = parts_ref.shape
    half = grad_ref.shape[0] // cores
    biases = []
    for core in range(cores):
        for place in range(plane):
            block = parts_ref[core, place].astype(f32)
            grad_ref[core * half : (core + 1) * half, place * lanes : (place + 1) * lanes] = block[
                :half
            ]
            if place == 0:
                biases.append(block[half : half + 1, :half])
    bias_ref[...] = jnp.concatenate(biases, axis=1)


def run(kernel, name, out_shape, args, specs, scratch=()):
    vmem = pl.BlockSpec(memory_space=pltpu.VMEM)
    smem = pl.BlockSpec(memory_space=pltpu.SMEM)
    kinds = {"v": vmem, "s": smem, "a": pl.BlockSpec(memory_space=pl.ANY)}
    return pl.pallas_call(
        kernel,
        out_shape=out_shape,
        in_specs=[kinds[spec] for spec in specs],
        out_specs=(vmem,) * len(out_shape),
        scratch_shapes=list(scratch),
        compiler_params=pltpu.CompilerParams(vmem_limit_bytes=(56 if scratch else 40) << 20),
        name=name,
    )(*args)


def on_device(
    features,
    tile_slide,
    tile_pos,
    slide_owner,
    slide_label,
    enc_weight,
    enc_bias,
    norm_gain,
    qkv_weight,
    out_weight,
    cls_weight,
):
    far_count = lax.axis_size(FAR)
    near_count = lax.axis_size(NEAR)
    groups = lax.axis_size("x")
    tile_count, _, channels = features.shape
    cols = enc_weight.shape[1]
    emb = cols * groups
    slot_total = far_count * near_count * SLOTS
    group_at = lax.axis_index("x")
    owner_at = lax.axis_index(ENC)

    shape = jax.ShapeDtypeStruct
    place = jnp.stack([group_at, owner_at, lax.axis_index("c")]).astype(jnp.int32)
    width = 3 * cols + 2 * CLASSES

    with jax.named_scope("encode"):
        own_rows = qkv_weight.shape[0]
        width_blocks = width // LANES
        sources = (
            tile_slide.reshape(1, tile_count),
            tile_pos[None, :],
            slide_owner[None, :],
            qkv_weight,
            out_weight,
            cls_weight.T,
            enc_bias[None, :],
            enc_weight.T,
            features,
        )
        send, mask, placing = run(
            send_kernel,
            "send",
            (
                shape((far_count, 24 + held_rows(width_blocks, own_rows), LANES), bf16),
                shape((tile_count * POS, cols), bf16),
                shape((slot_total, tile_count), bf16),
            ),
            (group_at.astype(jnp.int32)[None],) + sources,
            "s" + "a" * len(sources),
            [pltpu.VMEM(source.shape, source.dtype) for source in sources]
            + [pltpu.SemaphoreType.DMA((len(sources),))],
        )

    with jax.named_scope("dispatch"):
        send_near, far_held = run(
            functools.partial(turn_kernel, own_rows),
            "turn",
            (
                shape((groups, near_count, far_count * SLOTS, BLOCK), bf16),
                shape((width_blocks * far_count * own_rows, LANES), bf16),
            ),
            (swap(send, FAR),),
            "v",
        )
        rows = swap(
            send_near.reshape(groups * near_count, far_count * SLOTS, BLOCK), ("x",) + NEAR
        ).reshape(groups, slot_total, BLOCK)

    with jax.named_scope("weights"):
        weights = lax.all_gather(far_held, NEAR, axis=0)

    with jax.named_scope("attend"):
        gain = norm_gain.reshape(groups, 1, cols)
        cls_parts = cls_weight.T.reshape(CLASSES, groups, cols).transpose(1, 0, 2)
        part_logits, att, qkv, ordered = run(
            functools.partial(forward_kernel, own_rows),
            "forward",
            (
                shape((1, CLASSES), f32),
                shape((cols // HD, slot_total, slot_total), f32),
                shape((slot_total, 3 * cols), bf16),
                shape((groups, cols, width), bf16),
            ),
            (place, rows, weights, gain, cls_parts),
            "svvvv",
        )
        all_logits = lax.all_gather(part_logits, "x", axis=0)
        logits, grad_parts = run(
            backward_kernel,
            "backward",
            (
                shape((1, CLASSES), f32),
                shape((groups, near_count, far_count * SLOTS * 3 // 2, LANES), bf16),
            ),
            (
                place,
                all_logits,
                slide_owner[None, :],
                slide_label[None, :],
                rows,
                ordered,
                gain,
                cls_parts,
                att,
                qkv,
            ),
            "svvvvvvvvv",
        )

    with jax.named_scope("give_back"):
        from_near = swap(
            grad_parts.reshape((groups * near_count,) + grad_parts.shape[2:]), ("x",) + NEAR
        ).reshape(grad_parts.shape)
        (folded,) = run(
            fold_kernel, "fold", (shape((far_count, 24, LANES), bf16),), (from_near,), "v"
        )
        back_rows = swap(folded, FAR)

    with jax.named_scope("encoder_grad"):
        plane_count = lax.axis_size(PLANE)
        block = (cols // 2 + 8, channels // plane_count)
        operands = (place, placing, back_rows, mask, features)
        (sent,) = run(
            functools.partial(weight_grad_kernel, True),
            "other_half",
            (shape((plane_count,) + block, bf16),),
            operands,
            "svvvv",
        )
        other = lax.ppermute(sent, "c", [(0, 1), (1, 0)])
        (kept,) = run(
            functools.partial(weight_grad_kernel, False),
            "own_half",
            (shape((plane_count,) + block, bf16),),
            operands,
            "svvvv",
        )

    with jax.named_scope("reduce"):
        core_sum = (kept.astype(f32) + other.astype(f32)).astype(bf16)
        plane_sum = jnp.sum(swap_plane(core_sum).astype(f32), axis=0).astype(bf16)
        total = jnp.sum(gather_copies(plane_sum, "zh").astype(f32), axis=0).astype(bf16)
        copies = jnp.broadcast_to(total[None], (plane_count,) + total.shape)
        all_parts = lax.all_gather(swap_plane(copies), "c", axis=0)
        enc_grad, bias_grad = run(
            unpack_kernel,
            "unpack",
            (shape((cols, channels), f32), shape((1, cols), f32)),
            (all_parts,),
            "v",
        )
    return (logits, enc_grad.T, bias_grad[0])


def solution(mesh):
    enc_count, groups = mesh.devices.shape
    far_count = enc_count // 8
    far_lanes = 4 if far_count >= 16 else far_count // 2
    shape = (4, far_count // far_lanes, far_lanes, 2, groups)
    split = Mesh(mesh.devices.reshape(shape), ENC + ("x",))
    return jax.shard_map(
        on_device,
        mesh=split,
        in_specs=(
            P(ENC, None, None),
            P(ENC, None),
            P(ENC),
            P(),
            P(),
            P(None, "x"),
            P("x"),
            P(),
            P(ENC, None),
            P(ENC, None),
            P(),
        ),
        out_specs=(P(ENC, None), P(None, "x"), P("x")),
        check_vma=False,
    )
```

```python
import functools

import jax
import jax.numpy as jnp
from jax import lax
from jax.experimental import pallas as pl
from jax.experimental.pallas import tpu as pltpu
from jax.sharding import Mesh, PartitionSpec as P

POS = 4
HEADS = 12
CLASSES = 32
HD = 64
SLOTS = 2
BLOCK = 256
LANES = 128
FAR = ("zh", "zl")
ENC = ("y", "zh", "zl", "c")
NEAR = ("y", "c")
PLANE = ("y", "zl")
eps = 1e-05

bf16 = jnp.bfloat16
f32 = jnp.float32
EXACT = lax.Precision.HIGHEST


def across(lhs, rhs, dims, precision=None):
    return lax.dot_general(
        lhs, rhs, ((dims[:1], dims[1:]), ((), ())), precision=precision, preferred_element_type=f32
    )


def swap(blocks, axes):
    return lax.all_to_all(blocks, axes, split_axis=0, concat_axis=0, tiled=True)


def plane_groups():
    lines, far_count, cores = 4, lax.axis_size(FAR), 2
    length = lax.axis_size("zl")
    groups = []
    for core in range(cores):
        for first in range(0, far_count, length):
            stretch = [(first + core * length // 2 + at) % far_count for at in range(length)]
            groups.append(
                [(line * far_count + far) * cores + core for line in range(lines) for far in stretch]
            )
    return groups


def swap_plane(blocks):
    return lax.all_to_all(
        blocks, ENC, split_axis=0, concat_axis=0, axis_index_groups=plane_groups(), tiled=True
    )


def gather_copies(block, axes):
    return swap(jnp.broadcast_to(block[None], (lax.axis_size(axes),) + block.shape), axes)


def sum_blocks(blocks, axes):
    return jnp.sum(swap(blocks, axes).astype(f32), axis=0).astype(bf16)


def normed_parts(rows_ref, cols):
    parts = [
        rows_ref[part, :, :cols].astype(f32)
        for part in range(rows_ref.shape[0])
    ]
    width = cols * len(parts)
    mean = sum(jnp.sum(part, axis=1, keepdims=True) for part in parts) / width
    centred = [part - mean for part in parts]
    variance = sum(jnp.sum(part * part, axis=1, keepdims=True) for part in centred) / width
    inv_std = lax.rsqrt(variance + eps)
    return parts, [part * inv_std for part in centred], inv_std


def forward_kernel(
    own_rows,
    place_ref,
    rows_ref,
    weight_ref,
    gain_ref,
    cls_ref,
    logits_ref,
    att_ref,
    qkv_ref,
    weights_ref,
):
    groups, slots, _ = rows_ref.shape
    cols = gain_ref.shape[2]
    parts, normed, _ = normed_parts(rows_ref, cols)
    size = weight_ref.shape[1] // (-(-(3 * cols + 2 * CLASSES) // LANES))
    order = held_order(own_rows, cols)
    qkv = 0.0
    for part in range(groups):
        normed_in = (normed[part] * gain_ref[part]).astype(bf16)
        block = across(order, weight_block(weight_ref, part, size), (1, 0)).astype(bf16)
        weights_ref[part] = block
        qkv = qkv + across(normed_in, block, (1, 0))
    qkv = qkv[:, : 3 * cols]
    column = lax.broadcasted_iota(jnp.int32, (slots, 3 * cols), 1)
    qkv = jnp.where(column < cols, qkv * HD ** (-0.5), qkv).astype(bf16)
    qkv_ref[...] = qkv
    tags = rows_ref[0, :, cols : cols + 1].astype(f32)
    count = jnp.sum(tags, axis=0, keepdims=True) * 0.0 + jnp.sum(
        (tags > 0).astype(f32), axis=0, keepdims=True
    )
    down = lax.broadcasted_iota(jnp.int32, (slots, slots), 0)
    along = lax.broadcasted_iota(jnp.int32, (slots, slots), 1)
    tag_row = jnp.sum(jnp.where(down == along, tags, 0.0), axis=0, keepdims=True)
    query_pos = tags.astype(jnp.int32) - 1
    key_pos = tag_row.astype(jnp.int32) - 1
    wc = class_block(weights_ref, place_ref, cols)
    mixed = []
    for head in range(cols // HD):
        group = head % 3
        low = (1 << group) - 1
        query_key = ((query_pos >> (6 + group)) << group) + (query_pos & low)
        key_key = ((key_pos >> (6 + group)) << group) + (key_pos & low)
        query_key = jnp.where(query_pos < 0, -1, query_key)
        key_key = jnp.where(key_pos < 0, -2, key_key)
        visible = query_key == key_key
        first = head * HD
        scores = across(
            qkv[:, first : first + HD], qkv[:, cols + first : cols + first + HD], (1, 1)
        )
        masked = jnp.where(visible, scores, -1e30)
        row_max = jnp.max(masked, axis=1, keepdims=True)
        weights = jnp.where(visible, jnp.exp(masked - row_max), 0.0)
        row_total = jnp.sum(weights, axis=1, keepdims=True)
        att = weights / jnp.where(row_total > 0, row_total, 1.0)
        att_ref[head] = att
        att_total = jnp.sum(att.astype(bf16).astype(f32), axis=0, keepdims=True)
        values = qkv[:, 2 * cols + first : 2 * cols + first + HD]
        mixed.append(across(in_terms(att_total), values, (1, 0)))
    mixed_total = jnp.sum(jnp.concatenate(mixed, axis=1), axis=0, keepdims=True)
    total = fine(mixed_total, wc, (1, 0))
    for part in range(groups):
        row_sum = jnp.sum(parts[part], axis=0, keepdims=True) * (1.0 / groups)
        total = total + fine(row_sum, cls_ref[part], (1, 1))
    logits_ref[...] = total / count


def backward_kernel(
    place_ref,
    part_logits_ref,
    owner_ref,
    label_ref,
    rows_ref,
    weights_ref,
    gain_ref,
    cls_ref,
    att_ref,
    qkv_ref,
    logits_ref,
    grad_ref,
):
    groups, slots, _ = rows_ref.shape
    cols = gain_ref.shape[2]
    _, normed, inv_std = normed_parts(rows_ref, cols)
    tags = rows_ref[0, :, cols : cols + 1].astype(f32)
    live = (tags > 0).astype(f32)
    count = jnp.sum(live, axis=0, keepdims=True)
    logits = sum(part_logits_ref[part] for part in range(groups))
    logits_ref[...] = logits
    scaled = jnp.exp(logits - jnp.max(logits, axis=1, keepdims=True))
    class_probs = scaled / jnp.sum(scaled, axis=1, keepdims=True)
    mine = owner_ref[...] == place_ref[1]
    my_label = jnp.sum(jnp.where(mine, label_ref[...], 0).astype(f32), axis=1, keepdims=True)
    class_ids = lax.broadcasted_iota(jnp.int32, (1, CLASSES), 1).astype(f32)
    grad_logits = (class_probs - (class_ids == my_label).astype(f32)) / count
    wc = class_block(weights_ref, place_ref, cols)
    grad_mixed = fine(grad_logits, wc, (1, 1)).astype(bf16)
    qkv = qkv_ref[...]
    grad_q, grad_k, grad_v = [], [], []
    for head in range(cols // HD):
        first = head * HD
        att = att_ref[head]
        queries = qkv[:, first : first + HD]
        keys = qkv[:, cols + first : cols + first + HD]
        values = qkv[:, 2 * cols + first : 2 * cols + first + HD]
        head_grad = grad_mixed[:, first : first + HD]
        grad_att = across(head_grad, values, (1, 1))
        expected = jnp.sum(att * grad_att, axis=1, keepdims=True)
        grad_scores = (att * (grad_att - expected)).astype(bf16)
        grad_q.append(across(grad_scores, keys, (1, 0)) * HD ** (-0.5))
        grad_k.append(across(grad_scores, queries, (0, 0)))
        spread = jnp.broadcast_to(head_grad, (slots, HD))
        grad_v.append(across(att.astype(bf16), spread, (0, 0)))
    unused = jnp.zeros((slots, 2 * CLASSES), f32)
    grad_qkv = jnp.concatenate(grad_q + grad_k + grad_v + [unused], axis=1).astype(bf16)
    scaled_parts = []
    for part in range(groups):
        grad_normed = across(grad_qkv, weights_ref[part], (1, 1))
        scaled_parts.append(grad_normed * gain_ref[part])
    width = cols * groups
    mean = sum(jnp.sum(e, axis=1, keepdims=True) for e in scaled_parts) / width
    slope = (
        sum(jnp.sum(e * n, axis=1, keepdims=True) for e, n in zip(scaled_parts, normed)) / width
    )
    for part in range(groups):
        pooled = fine(grad_logits, cls_ref[part], (1, 0)) * (1.0 / groups)
        grad = inv_std * (scaled_parts[part] - mean - normed[part] * slope)
        folded = fold_rows(live * pooled + grad, grad_ref.shape[0]).astype(bf16)
        for near in range(grad_ref.shape[0]):
            grad_ref[near, part] = folded[near]


def as_column(row):
    size = row.shape[1]
    down = lax.broadcasted_iota(jnp.int32, (size, size), 0)
    along = lax.broadcasted_iota(jnp.int32, (size, size), 1)
    return jnp.sum(jnp.where(down == along, row, 0.0), axis=1, keepdims=True)


def in_terms(row):
    high = row.astype(bf16)
    rest = row - high.astype(f32)
    middle = rest.astype(bf16)
    low = (rest - middle.astype(f32)).astype(bf16)
    terms = [term.astype(f32) for term in (high, middle, low)]
    return jnp.concatenate(terms + [jnp.zeros((5, row.shape[1]), f32)], axis=0).astype(bf16)


def fine(row, matrix, dims):
    terms = in_terms(row)
    high = matrix.astype(bf16)
    low = (matrix - high.astype(f32)).astype(bf16)
    summed = across(terms, high, dims) + across(terms, low, dims)
    return jnp.sum(summed, axis=0, keepdims=True)


def held_rows(blocks, rows):
    return (blocks * rows + 8) // 8 * 8


def fold_rows(rows, count):
    blocks = rows.reshape(count, rows.shape[0] // count, rows.shape[1])
    half = blocks.shape[1] // 2
    rest = jnp.concatenate([blocks[:, :half, LANES:], blocks[:, half:, LANES:]], axis=2)
    return jnp.concatenate([blocks[:, :, :LANES], rest], axis=1)


def unfold_rows(blocks, size):
    rest = blocks[:, size : size + size // 2]
    half = LANES // 2
    rest = jnp.concatenate([rest[:, :, :half], rest[:, :, half:]], axis=1)
    total = blocks.shape[0] * size
    return blocks[:, :size].reshape(total, LANES), rest.reshape(total, half)


def slot_order(far_bits, slots):
    at = lax.broadcasted_iota(jnp.int32, (slots, slots), 0)
    source = lax.broadcasted_iota(jnp.int32, (slots, slots), 1)
    near = at >> (far_bits + 1)
    far = (at >> 1) & ((1 << far_bits) - 1)
    return (source == far * 16 + near * 2 + (at & 1)).astype(f32).astype(bf16)


def send_kernel(place_ref, *refs):
    sources, refs = refs[:9], refs[9:]
    send_ref, mask_ref, placing_ref = refs[:3]
    targets, sems = refs[3:12], refs[12]
    copies = [
        pltpu.make_async_copy(source, target, sems.at[number])
        for number, (source, target) in enumerate(zip(sources, targets))
    ]
    for copy in copies:
        copy.start()
    slide_ref, pos_ref, owner_ref, qkv_ref, out_ref, cls_ref = targets[:6]
    bias_ref, weight_ref, features_ref = targets[6:]
    for copy in copies:
        copy.wait()
    tiles, positions, channels = features_ref.shape
    far_count = send_ref.shape[0]
    cols = weight_ref.shape[0]
    slides = owner_ref.shape[1]

    slide_row = slide_ref[...]
    owner_column = as_column(owner_ref[...].astype(f32))
    slide_ids = lax.broadcasted_iota(jnp.int32, (slides, tiles), 0)
    owners = jnp.sum(
        jnp.where(slide_ids == slide_row, owner_column, 0.0), axis=0, keepdims=True
    ).astype(jnp.int32)
    slide_values = slide_row.astype(f32)
    down = lax.broadcasted_iota(jnp.int32, (tiles, tiles), 0)
    along = lax.broadcasted_iota(jnp.int32, (tiles, tiles), 1)
    earlier = (as_column(slide_values) == slide_values) & (down < along)
    slot_rank = jnp.sum(earlier.astype(f32), axis=0, keepdims=True).astype(jnp.int32)
    owner_pair = owners >> 1
    line = sum((owner_pair >= far_count * number).astype(jnp.int32) for number in range(1, 4))
    near_owner = line * 2 + (owners & 1)
    far_owner = owner_pair - line * far_count
    target = (far_owner * 8 + near_owner) * SLOTS + slot_rank
    slots = lax.broadcasted_iota(jnp.int32, placing_ref.shape, 0)
    placing = slots == target
    tags = jnp.sum(
        jnp.where(placing, (pos_ref[...] + 1).astype(f32), 0.0), axis=1, keepdims=True
    )
    placing = placing.astype(f32).astype(bf16)
    placing_ref[...] = placing
    slot_ids = lax.broadcasted_iota(jnp.int32, (far_count * 16, LANES), 0)
    lane_ids = lax.broadcasted_iota(jnp.int32, (far_count * 16, LANES), 1)
    tag_rows = jnp.where(lane_ids == (slot_ids & 15), tags, 0.0)
    tag_rows = jnp.sum(tag_rows.reshape(far_count, 16, LANES), axis=1)

    own_rows, emb = out_ref.shape
    wc = across(out_ref[...].astype(f32), cls_ref[...], (1, 1), EXACT)
    wc_high = wc.astype(bf16).astype(f32)
    picked = []
    for part in range(3):
        block = qkv_ref[:, part * emb : part * emb + cols]
        for group in range(1, emb // cols):
            first = part * emb + group * cols
            block = jnp.where(place_ref[0] == group, qkv_ref[:, first : first + cols], block)
        picked.append(block.astype(f32))
    rows = jnp.concatenate(picked + [wc_high, wc - wc_high], axis=1)
    held = [rows[:, at : at + LANES] for at in range(0, rows.shape[1], LANES)]
    tag_at = len(held) * own_rows
    padded = held_rows(len(held), own_rows)
    held = jnp.concatenate(held + [jnp.zeros((padded - tag_at, LANES), f32)], axis=0)
    is_tag = lax.broadcasted_iota(jnp.int32, (padded, LANES), 0) == tag_at
    flattened = features_ref[...].reshape(tiles * positions, channels)
    preact = across(flattened, weight_ref[...], (1, 1)) + bias_ref[...]
    mask_ref[...] = jnp.where(preact > 0, 1.0 / positions, 0.0).astype(bf16)
    summed = jnp.sum(jnp.maximum(preact, 0.0).reshape(tiles, positions, cols), axis=1)
    tile_rows = (summed * (1.0 / positions)).astype(bf16)
    blocks = fold_rows(across(placing, tile_rows, (1, 0)), far_count)
    for far in range(far_count):
        rest = jnp.where(is_tag, tag_rows[far : far + 1], held)
        send_ref[far] = jnp.concatenate([blocks[far], rest], axis=0).astype(bf16)


def turn_kernel(own_rows, received_ref, rows_ref, held_ref):
    far_count = received_ref.shape[0]
    slots = far_count * 16
    far_bits = far_count.bit_length() - 1
    received = received_ref[...].astype(f32)
    order = slot_order(far_bits, slots)
    wide, narrow = unfold_rows(received, 16)
    wide = across(order, wide.astype(bf16), (1, 0))
    narrow = across(order, narrow.astype(bf16), (1, 0))
    slot = lax.broadcasted_iota(jnp.int32, (slots, far_count), 0)
    far = lax.broadcasted_iota(jnp.int32, (slots, far_count), 1)
    from_far = (((slot >> 1) & (far_count - 1)) == far).astype(f32).astype(bf16)
    size = far_count * own_rows
    block_count = held_ref.shape[0] // size
    tag_rows = received[:, 24 + block_count * own_rows].astype(bf16)
    slot = lax.broadcasted_iota(jnp.int32, (slots, LANES), 0)
    lane = lax.broadcasted_iota(jnp.int32, (slots, LANES), 1)
    mine = lane == (slot >> (far_bits + 1)) * 2 + (slot & 1)
    tags = jnp.sum(
        jnp.where(mine, across(from_far, tag_rows, (1, 0)), 0.0), axis=1, keepdims=True
    )
    tags = jnp.broadcast_to(tags, (slots, LANES // 2))
    rows = jnp.concatenate([wide, narrow, tags], axis=1).astype(bf16)
    rows = rows.reshape(rows_ref.shape[1:])
    for group in range(rows_ref.shape[0]):
        rows_ref[group] = rows
    padded = received.shape[1] - 24
    held = received[:, 24:].reshape(far_count * padded, LANES).astype(bf16)
    row = lax.broadcasted_iota(jnp.int32, (size, 1), 0).astype(f32)
    column = lax.broadcasted_iota(jnp.int32, (size, far_count * padded), 1)
    far = jnp.floor((row + 0.5) * (1.0 / own_rows))
    source = (row + far * (padded - own_rows)).astype(jnp.int32)
    for block in range(block_count):
        kept = (column == source + block * own_rows).astype(f32).astype(bf16)
        held_ref[block * size : (block + 1) * size] = across(kept, held, (1, 0)).astype(bf16)


def fold_kernel(parts_ref, back_ref):
    groups = parts_ref.shape[1]
    far_count = back_ref.shape[0]
    total = sum(parts_ref[:, group].astype(f32) for group in range(groups))
    wide, narrow = unfold_rows(total, far_count * SLOTS)
    total = jnp.concatenate([wide, narrow], axis=1).astype(bf16)
    order = slot_order(far_count.bit_length() - 1, total.shape[0])
    back_ref[...] = fold_rows(across(order, total, (0, 0)), far_count).astype(bf16)


def held_order(own_rows, cols):
    row = lax.broadcasted_iota(jnp.int32, (cols, cols), 0)
    place = lax.broadcasted_iota(jnp.int32, (1, cols), 1).astype(f32)
    block = jnp.floor((place + 0.5) * (1.0 / own_rows))
    far_count = cols // (2 * own_rows)
    core = (block >= far_count).astype(f32)
    source = place + (block - core * far_count + core - core * far_count) * own_rows
    return (row == source.astype(jnp.int32)).astype(f32).astype(bf16)


def weight_block(weight_ref, part, size):
    columns = []
    for block in range(weight_ref.shape[1] // size):
        pair = [
            weight_ref[part * 2 + core, block * size : (block + 1) * size] for core in range(2)
        ]
        columns.append(jnp.concatenate(pair, axis=0))
    return jnp.concatenate(columns, axis=1)


def class_block(weights_ref, place_ref, cols):
    mine = weights_ref[place_ref[0]]
    both = mine[:, 3 * cols :].astype(f32)
    return both[:, :CLASSES] + both[:, CLASSES : 2 * CLASSES]


def weight_grad_kernel(
    of_other, place_ref, placing_ref, back_ref, mask_ref, features_ref, half_ref
):
    tiles, positions, channels = features_ref.shape
    half = mask_ref.shape[1] // 2
    is_first = place_ref[2] == (1 if of_other else 0)
    back = jnp.concatenate(unfold_rows(back_ref[...].astype(f32), 16), axis=1)
    back = jnp.where(is_first, back[:, :half], back[:, half:]).astype(bf16)
    mask = mask_ref[...].astype(f32)
    mask = jnp.where(is_first, mask[:, :half], mask[:, half:])
    tile_grads = across(placing_ref[...], back, (0, 0))
    spread = jnp.broadcast_to(tile_grads[:, None, :], (tiles, positions, half))
    grad_preact = spread.reshape(tiles * positions, half) * mask
    bias = jnp.sum(grad_preact, axis=0, keepdims=True)
    flattened = features_ref[...].reshape(tiles * positions, channels)
    grad = across(grad_preact.astype(bf16), flattened, (0, 0))
    lanes = channels // half_ref.shape[0]
    bias_rows = jnp.concatenate([bias, jnp.zeros((1, lanes - half), f32)], axis=1)
    bias_rows = jnp.broadcast_to(bias_rows, (8, lanes))
    for place in range(half_ref.shape[0]):
        block = grad[:, place * lanes : (place + 1) * lanes]
        half_ref[place] = jnp.concatenate([block, bias_rows], axis=0).astype(bf16)


def unpack_kernel(parts_ref, grad_ref, bias_ref):
    cores, plane, _, lanes = parts_ref.shape
    half = grad_ref.shape[0] // cores
    biases = []
    for core in range(cores):
        for place in range(plane):
            block = parts_ref[core, place].astype(f32)
            grad_ref[core * half : (core + 1) * half, place * lanes : (place + 1) * lanes] = block[
                :half
            ]
            if place == 0:
                biases.append(block[half : half + 1, :half])
    bias_ref[...] = jnp.concatenate(biases, axis=1)


def run(kernel, name, out_shape, args, specs, scratch=()):
    vmem = pl.BlockSpec(memory_space=pltpu.VMEM)
    smem = pl.BlockSpec(memory_space=pltpu.SMEM)
    kinds = {"v": vmem, "s": smem, "a": pl.BlockSpec(memory_space=pl.ANY)}
    return pl.pallas_call(
        kernel,
        out_shape=out_shape,
        in_specs=[kinds[spec] for spec in specs],
        out_specs=(vmem,) * len(out_shape),
        scratch_shapes=list(scratch),
        compiler_params=pltpu.CompilerParams(vmem_limit_bytes=(56 if scratch else 40) << 20),
        name=name,
    )(*args)


def on_device(
    features,
    tile_slide,
    tile_pos,
    slide_owner,
    slide_label,
    enc_weight,
    enc_bias,
    norm_gain,
    qkv_weight,
    out_weight,
    cls_weight,
):
    far_count = lax.axis_size(FAR)
    near_count = lax.axis_size(NEAR)
    groups = lax.axis_size("x")
    tile_count, _, channels = features.shape
    cols = enc_weight.shape[1]
    emb = cols * groups
    slot_total = far_count * near_count * SLOTS
    group_at = lax.axis_index("x")
    owner_at = lax.axis_index(ENC)

    shape = jax.ShapeDtypeStruct
    place = jnp.stack([group_at, owner_at, lax.axis_index("c")]).astype(jnp.int32)
    width = 3 * cols + 2 * CLASSES

    with jax.named_scope("encode"):
        own_rows = qkv_weight.shape[0]
        width_blocks = width // LANES
        sources = (
            tile_slide.reshape(1, tile_count),
            tile_pos[None, :],
            slide_owner[None, :],
            qkv_weight,
            out_weight,
            cls_weight.T,
            enc_bias[None, :],
            enc_weight.T,
            features,
        )
        send, mask, placing = run(
            send_kernel,
            "send",
            (
                shape((far_count, 24 + held_rows(width_blocks, own_rows), LANES), bf16),
                shape((tile_count * POS, cols), bf16),
                shape((slot_total, tile_count), bf16),
            ),
            (group_at.astype(jnp.int32)[None],) + sources,
            "s" + "a" * len(sources),
            [pltpu.VMEM(source.shape, source.dtype) for source in sources]
            + [pltpu.SemaphoreType.DMA((len(sources),))],
        )

    with jax.named_scope("dispatch"):
        send_near, far_held = run(
            functools.partial(turn_kernel, own_rows),
            "turn",
            (
                shape((groups, near_count, far_count * SLOTS, BLOCK), bf16),
                shape((width_blocks * far_count * own_rows, LANES), bf16),
            ),
            (swap(send, FAR),),
            "v",
        )
        rows = swap(
            send_near.reshape(groups * near_count, far_count * SLOTS, BLOCK), ("x",) + NEAR
        ).reshape(groups, slot_total, BLOCK)

    with jax.named_scope("weights"):
        weights = lax.all_gather(far_held, NEAR, axis=0)

    with jax.named_scope("attend"):
        gain = norm_gain.reshape(groups, 1, cols)
        cls_parts = cls_weight.T.reshape(CLASSES, groups, cols).transpose(1, 0, 2)
        part_logits, att, qkv, ordered = run(
            functools.partial(forward_kernel, own_rows),
            "forward",
            (
                shape((1, CLASSES), f32),
                shape((cols // HD, slot_total, slot_total), f32),
                shape((slot_total, 3 * cols), bf16),
                shape((groups, cols, width), bf16),
            ),
            (place, rows, weights, gain, cls_parts),
            "svvvv",
        )
        all_logits = lax.all_gather(part_logits, "x", axis=0)
        logits, grad_parts = run(
            backward_kernel,
            "backward",
            (
                shape((1, CLASSES), f32),
                shape((near_count, groups, far_count * SLOTS * 3 // 2, LANES), bf16),
            ),
            (
                place,
                all_logits,
                slide_owner[None, :],
                slide_label[None, :],
                rows,
                ordered,
                gain,
                cls_parts,
                att,
                qkv,
            ),
            "svvvvvvvvv",
        )

    with jax.named_scope("give_back"):
        from_near = swap(
            grad_parts.reshape((groups * near_count,) + grad_parts.shape[2:]), NEAR + ("x",)
        ).reshape(grad_parts.shape)
        (folded,) = run(
            fold_kernel, "fold", (shape((far_count, 24, LANES), bf16),), (from_near,), "v"
        )
        back_rows = swap(folded, FAR)

    with jax.named_scope("encoder_grad"):
        plane_count = lax.axis_size(PLANE)
        block = (cols // 2 + 8, channels // plane_count)
        operands = (place, placing, back_rows, mask, features)
        (sent,) = run(
            functools.partial(weight_grad_kernel, True),
            "other_half",
            (shape((plane_count,) + block, bf16),),
            operands,
            "svvvv",
        )
        other = lax.ppermute(sent, "c", [(0, 1), (1, 0)])
        (kept,) = run(
            functools.partial(weight_grad_kernel, False),
            "own_half",
            (shape((plane_count,) + block, bf16),),
            operands,
            "svvvv",
        )

    with jax.named_scope("reduce"):
        core_sum = (kept.astype(f32) + other.astype(f32)).astype(bf16)
        plane_sum = jnp.sum(swap_plane(core_sum).astype(f32), axis=0).astype(bf16)
        total = jnp.sum(gather_copies(plane_sum, "zh").astype(f32), axis=0).astype(bf16)
        copies = jnp.broadcast_to(total[None], (plane_count,) + total.shape)
        all_parts = lax.all_gather(swap_plane(copies), "c", axis=0)
        enc_grad, bias_grad = run(
            unpack_kernel,
            "unpack",
            (shape((cols, channels), f32), shape((1, cols), f32)),
            (all_parts,),
            "v",
        )
    return (logits, enc_grad.T, bias_grad[0])


def solution(mesh):
    enc_count, groups = mesh.devices.shape
    far_count = enc_count // 8
    far_lanes = 4 if far_count >= 16 else far_count // 2
    shape = (4, far_count // far_lanes, far_lanes, 2, groups)
    split = Mesh(mesh.devices.reshape(shape), ENC + ("x",))
    return jax.shard_map(
        on_device,
        mesh=split,
        in_specs=(
            P(ENC, None, None),
            P(ENC, None),
            P(ENC),
            P(),
            P(),
            P(None, "x"),
            P("x"),
            P(),
            P(ENC, None),
            P(ENC, None),
            P(),
        ),
        out_specs=(P(ENC, None), P(None, "x"), P("x")),
        check_vma=False,
    )
```

```python
import functools

import jax
import jax.numpy as jnp
from jax import lax
from jax.experimental import pallas as pl
from jax.experimental.pallas import tpu as pltpu
from jax.sharding import Mesh, PartitionSpec as P

POS = 4
HEADS = 12
CLASSES = 32
HD = 64
SLOTS = 2
BLOCK = 256
LANES = 128
FAR = ("zh", "zl")
ENC = ("y", "zh", "zl", "c")
NEAR = ("y", "c")
PLANE = ("y", "zl")
eps = 1e-05

bf16 = jnp.bfloat16
f32 = jnp.float32
EXACT = lax.Precision.HIGHEST


def across(lhs, rhs, dims, precision=None):
    return lax.dot_general(
        lhs, rhs, ((dims[:1], dims[1:]), ((), ())), precision=precision, preferred_element_type=f32
    )


def swap(blocks, axes):
    return lax.all_to_all(blocks, axes, split_axis=0, concat_axis=0, tiled=True)


def plane_groups():
    lines, far_count, cores = 4, lax.axis_size(FAR), 2
    length = lax.axis_size("zl")
    groups = []
    for core in range(cores):
        for first in range(0, far_count, length):
            stretch = [(first + core * length // 2 + at) % far_count for at in range(length)]
            groups.append(
                [(line * far_count + far) * cores + core for far in stretch for line in range(lines)]
            )
    return groups


def swap_plane(blocks):
    return lax.all_to_all(
        blocks, ENC, split_axis=0, concat_axis=0, axis_index_groups=plane_groups(), tiled=True
    )


def gather_copies(block, axes):
    return swap(jnp.broadcast_to(block[None], (lax.axis_size(axes),) + block.shape), axes)


def sum_blocks(blocks, axes):
    return jnp.sum(swap(blocks, axes).astype(f32), axis=0).astype(bf16)


def normed_parts(rows_ref, cols):
    parts = [
        rows_ref[part, :, :cols].astype(f32)
        for part in range(rows_ref.shape[0])
    ]
    width = cols * len(parts)
    mean = sum(jnp.sum(part, axis=1, keepdims=True) for part in parts) / width
    centred = [part - mean for part in parts]
    variance = sum(jnp.sum(part * part, axis=1, keepdims=True) for part in centred) / width
    inv_std = lax.rsqrt(variance + eps)
    return parts, [part * inv_std for part in centred], inv_std


def forward_kernel(
    own_rows,
    place_ref,
    rows_ref,
    weight_ref,
    gain_ref,
    cls_ref,
    logits_ref,
    att_ref,
    qkv_ref,
    weights_ref,
):
    groups, slots, _ = rows_ref.shape
    cols = gain_ref.shape[2]
    parts, normed, _ = normed_parts(rows_ref, cols)
    size = weight_ref.shape[1] // (-(-(3 * cols + 2 * CLASSES) // LANES))
    order = held_order(own_rows, cols)
    qkv = 0.0
    for part in range(groups):
        normed_in = (normed[part] * gain_ref[part]).astype(bf16)
        block = across(order, weight_block(weight_ref, part, size), (1, 0)).astype(bf16)
        weights_ref[part] = block
        qkv = qkv + across(normed_in, block, (1, 0))
    qkv = qkv[:, : 3 * cols]
    column = lax.broadcasted_iota(jnp.int32, (slots, 3 * cols), 1)
    qkv = jnp.where(column < cols, qkv * HD ** (-0.5), qkv).astype(bf16)
    qkv_ref[...] = qkv
    tags = rows_ref[0, :, cols : cols + 1].astype(f32)
    count = jnp.sum(tags, axis=0, keepdims=True) * 0.0 + jnp.sum(
        (tags > 0).astype(f32), axis=0, keepdims=True
    )
    down = lax.broadcasted_iota(jnp.int32, (slots, slots), 0)
    along = lax.broadcasted_iota(jnp.int32, (slots, slots), 1)
    tag_row = jnp.sum(jnp.where(down == along, tags, 0.0), axis=0, keepdims=True)
    query_pos = tags.astype(jnp.int32) - 1
    key_pos = tag_row.astype(jnp.int32) - 1
    wc = class_block(weights_ref, place_ref, cols)
    mixed = []
    for head in range(cols // HD):
        group = head % 3
        low = (1 << group) - 1
        query_key = ((query_pos >> (6 + group)) << group) + (query_pos & low)
        key_key = ((key_pos >> (6 + group)) << group) + (key_pos & low)
        query_key = jnp.where(query_pos < 0, -1, query_key)
        key_key = jnp.where(key_pos < 0, -2, key_key)
        visible = query_key == key_key
        first = head * HD
        scores = across(
            qkv[:, first : first + HD], qkv[:, cols + first : cols + first + HD], (1, 1)
        )
        masked = jnp.where(visible, scores, -1e30)
        row_max = jnp.max(masked, axis=1, keepdims=True)
        weights = jnp.where(visible, jnp.exp(masked - row_max), 0.0)
        row_total = jnp.sum(weights, axis=1, keepdims=True)
        att = weights / jnp.where(row_total > 0, row_total, 1.0)
        att_ref[head] = att
        att_total = jnp.sum(att.astype(bf16).astype(f32), axis=0, keepdims=True)
        values = qkv[:, 2 * cols + first : 2 * cols + first + HD]
        mixed.append(across(in_terms(att_total), values, (1, 0)))
    mixed_total = jnp.sum(jnp.concatenate(mixed, axis=1), axis=0, keepdims=True)
    total = fine(mixed_total, wc, (1, 0))
    for part in range(groups):
        row_sum = jnp.sum(parts[part], axis=0, keepdims=True) * (1.0 / groups)
        total = total + fine(row_sum, cls_ref[part], (1, 1))
    logits_ref[...] = total / count


def backward_kernel(
    place_ref,
    part_logits_ref,
    owner_ref,
    label_ref,
    rows_ref,
    weights_ref,
    gain_ref,
    cls_ref,
    att_ref,
    qkv_ref,
    logits_ref,
    grad_ref,
):
    groups, slots, _ = rows_ref.shape
    cols = gain_ref.shape[2]
    _, normed, inv_std = normed_parts(rows_ref, cols)
    tags = rows_ref[0, :, cols : cols + 1].astype(f32)
    live = (tags > 0).astype(f32)
    count = jnp.sum(live, axis=0, keepdims=True)
    logits = sum(part_logits_ref[part] for part in range(groups))
    logits_ref[...] = logits
    scaled = jnp.exp(logits - jnp.max(logits, axis=1, keepdims=True))
    class_probs = scaled / jnp.sum(scaled, axis=1, keepdims=True)
    mine = owner_ref[...] == place_ref[1]
    my_label = jnp.sum(jnp.where(mine, label_ref[...], 0).astype(f32), axis=1, keepdims=True)
    class_ids = lax.broadcasted_iota(jnp.int32, (1, CLASSES), 1).astype(f32)
    grad_logits = (class_probs - (class_ids == my_label).astype(f32)) / count
    wc = class_block(weights_ref, place_ref, cols)
    grad_mixed = fine(grad_logits, wc, (1, 1)).astype(bf16)
    qkv = qkv_ref[...]
    grad_q, grad_k, grad_v = [], [], []
    for head in range(cols // HD):
        first = head * HD
        att = att_ref[head]
        queries = qkv[:, first : first + HD]
        keys = qkv[:, cols + first : cols + first + HD]
        values = qkv[:, 2 * cols + first : 2 * cols + first + HD]
        head_grad = grad_mixed[:, first : first + HD]
        grad_att = across(head_grad, values, (1, 1))
        expected = jnp.sum(att * grad_att, axis=1, keepdims=True)
        grad_scores = (att * (grad_att - expected)).astype(bf16)
        grad_q.append(across(grad_scores, keys, (1, 0)) * HD ** (-0.5))
        grad_k.append(across(grad_scores, queries, (0, 0)))
        spread = jnp.broadcast_to(head_grad, (slots, HD))
        grad_v.append(across(att.astype(bf16), spread, (0, 0)))
    unused = jnp.zeros((slots, 2 * CLASSES), f32)
    grad_qkv = jnp.concatenate(grad_q + grad_k + grad_v + [unused], axis=1).astype(bf16)
    scaled_parts = []
    for part in range(groups):
        grad_normed = across(grad_qkv, weights_ref[part], (1, 1))
        scaled_parts.append(grad_normed * gain_ref[part])
    width = cols * groups
    mean = sum(jnp.sum(e, axis=1, keepdims=True) for e in scaled_parts) / width
    slope = (
        sum(jnp.sum(e * n, axis=1, keepdims=True) for e, n in zip(scaled_parts, normed)) / width
    )
    for part in range(groups):
        pooled = fine(grad_logits, cls_ref[part], (1, 0)) * (1.0 / groups)
        grad = inv_std * (scaled_parts[part] - mean - normed[part] * slope)
        grad_ref[part] = fold_rows(live * pooled + grad, grad_ref.shape[1]).astype(bf16)


def as_column(row):
    size = row.shape[1]
    down = lax.broadcasted_iota(jnp.int32, (size, size), 0)
    along = lax.broadcasted_iota(jnp.int32, (size, size), 1)
    return jnp.sum(jnp.where(down == along, row, 0.0), axis=1, keepdims=True)


def in_terms(row):
    high = row.astype(bf16)
    rest = row - high.astype(f32)
    middle = rest.astype(bf16)
    low = (rest - middle.astype(f32)).astype(bf16)
    terms = [term.astype(f32) for term in (high, middle, low)]
    return jnp.concatenate(terms + [jnp.zeros((5, row.shape[1]), f32)], axis=0).astype(bf16)


def fine(row, matrix, dims):
    terms = in_terms(row)
    high = matrix.astype(bf16)
    low = (matrix - high.astype(f32)).astype(bf16)
    summed = across(terms, high, dims) + across(terms, low, dims)
    return jnp.sum(summed, axis=0, keepdims=True)


def held_rows(blocks, rows):
    return (blocks * rows + 8) // 8 * 8


def fold_rows(rows, count):
    blocks = rows.reshape(count, rows.shape[0] // count, rows.shape[1])
    half = blocks.shape[1] // 2
    rest = jnp.concatenate([blocks[:, :half, LANES:], blocks[:, half:, LANES:]], axis=2)
    return jnp.concatenate([blocks[:, :, :LANES], rest], axis=1)


def unfold_rows(blocks, size):
    rest = blocks[:, size : size + size // 2]
    half = LANES // 2
    rest = jnp.concatenate([rest[:, :, :half], rest[:, :, half:]], axis=1)
    total = blocks.shape[0] * size
    return blocks[:, :size].reshape(total, LANES), rest.reshape(total, half)


def slot_order(far_bits, slots):
    at = lax.broadcasted_iota(jnp.int32, (slots, slots), 0)
    source = lax.broadcasted_iota(jnp.int32, (slots, slots), 1)
    near = at >> (far_bits + 1)
    far = (at >> 1) & ((1 << far_bits) - 1)
    return (source == far * 16 + near * 2 + (at & 1)).astype(f32).astype(bf16)


def send_kernel(place_ref, *refs):
    sources, refs = refs[:9], refs[9:]
    send_ref, mask_ref, placing_ref = refs[:3]
    targets, sems = refs[3:12], refs[12]
    copies = [
        pltpu.make_async_copy(source, target, sems.at[number])
        for number, (source, target) in enumerate(zip(sources, targets))
    ]
    for copy in copies:
        copy.start()
    slide_ref, pos_ref, owner_ref, qkv_ref, out_ref, cls_ref = targets[:6]
    bias_ref, weight_ref, features_ref = targets[6:]
    for copy in copies:
        copy.wait()
    tiles, positions, channels = features_ref.shape
    far_count = send_ref.shape[0]
    cols = weight_ref.shape[0]
    slides = owner_ref.shape[1]

    slide_row = slide_ref[...]
    owner_column = as_column(owner_ref[...].astype(f32))
    slide_ids = lax.broadcasted_iota(jnp.int32, (slides, tiles), 0)
    owners = jnp.sum(
        jnp.where(slide_ids == slide_row, owner_column, 0.0), axis=0, keepdims=True
    ).astype(jnp.int32)
    slide_values = slide_row.astype(f32)
    down = lax.broadcasted_iota(jnp.int32, (tiles, tiles), 0)
    along = lax.broadcasted_iota(jnp.int32, (tiles, tiles), 1)
    earlier = (as_column(slide_values) == slide_values) & (down < along)
    slot_rank = jnp.sum(earlier.astype(f32), axis=0, keepdims=True).astype(jnp.int32)
    owner_pair = owners >> 1
    line = sum((owner_pair >= far_count * number).astype(jnp.int32) for number in range(1, 4))
    near_owner = line * 2 + (owners & 1)
    far_owner = owner_pair - line * far_count
    target = (far_owner * 8 + near_owner) * SLOTS + slot_rank
    slots = lax.broadcasted_iota(jnp.int32, placing_ref.shape, 0)
    placing = slots == target
    tags = jnp.sum(
        jnp.where(placing, (pos_ref[...] + 1).astype(f32), 0.0), axis=1, keepdims=True
    )
    placing = placing.astype(f32).astype(bf16)
    placing_ref[...] = placing
    slot_ids = lax.broadcasted_iota(jnp.int32, (far_count * 16, LANES), 0)
    lane_ids = lax.broadcasted_iota(jnp.int32, (far_count * 16, LANES), 1)
    tag_rows = jnp.where(lane_ids == (slot_ids & 15), tags, 0.0)
    tag_rows = jnp.sum(tag_rows.reshape(far_count, 16, LANES), axis=1)

    own_rows, emb = out_ref.shape
    wc = across(out_ref[...].astype(f32), cls_ref[...], (1, 1), EXACT)
    wc_high = wc.astype(bf16).astype(f32)
    picked = []
    for part in range(3):
        block = qkv_ref[:, part * emb : part * emb + cols]
        for group in range(1, emb // cols):
            first = part * emb + group * cols
            block = jnp.where(place_ref[0] == group, qkv_ref[:, first : first + cols], block)
        picked.append(block.astype(f32))
    rows = jnp.concatenate(picked + [wc_high, wc - wc_high], axis=1)
    held = [rows[:, at : at + LANES] for at in range(0, rows.shape[1], LANES)]
    tag_at = len(held) * own_rows
    padded = held_rows(len(held), own_rows)
    held = jnp.concatenate(held + [jnp.zeros((padded - tag_at, LANES), f32)], axis=0)
    is_tag = lax.broadcasted_iota(jnp.int32, (padded, LANES), 0) == tag_at
    flattened = features_ref[...].reshape(tiles * positions, channels)
    preact = across(flattened, weight_ref[...], (1, 1)) + bias_ref[...]
    mask_ref[...] = jnp.where(preact > 0, 1.0 / positions, 0.0).astype(bf16)
    summed = jnp.sum(jnp.maximum(preact, 0.0).reshape(tiles, positions, cols), axis=1)
    tile_rows = (summed * (1.0 / positions)).astype(bf16)
    blocks = fold_rows(across(placing, tile_rows, (1, 0)), far_count)
    for far in range(far_count):
        rest = jnp.where(is_tag, tag_rows[far : far + 1], held)
        send_ref[far] = jnp.concatenate([blocks[far], rest], axis=0).astype(bf16)


def turn_kernel(own_rows, received_ref, rows_ref, held_ref):
    far_count = received_ref.shape[0]
    slots = far_count * 16
    far_bits = far_count.bit_length() - 1
    received = received_ref[...].astype(f32)
    order = slot_order(far_bits, slots)
    wide, narrow = unfold_rows(received, 16)
    wide = across(order, wide.astype(bf16), (1, 0))
    narrow = across(order, narrow.astype(bf16), (1, 0))
    slot = lax.broadcasted_iota(jnp.int32, (slots, far_count), 0)
    far = lax.broadcasted_iota(jnp.int32, (slots, far_count), 1)
    from_far = (((slot >> 1) & (far_count - 1)) == far).astype(f32).astype(bf16)
    size = far_count * own_rows
    block_count = held_ref.shape[0] // size
    tag_rows = received[:, 24 + block_count * own_rows].astype(bf16)
    slot = lax.broadcasted_iota(jnp.int32, (slots, LANES), 0)
    lane = lax.broadcasted_iota(jnp.int32, (slots, LANES), 1)
    mine = lane == (slot >> (far_bits + 1)) * 2 + (slot & 1)
    tags = jnp.sum(
        jnp.where(mine, across(from_far, tag_rows, (1, 0)), 0.0), axis=1, keepdims=True
    )
    tags = jnp.broadcast_to(tags, (slots, LANES // 2))
    rows = jnp.concatenate([wide, narrow, tags], axis=1).astype(bf16)
    rows = rows.reshape(rows_ref.shape[1:])
    for group in range(rows_ref.shape[0]):
        rows_ref[group] = rows
    padded = received.shape[1] - 24
    held = received[:, 24:].reshape(far_count * padded, LANES).astype(bf16)
    row = lax.broadcasted_iota(jnp.int32, (size, 1), 0).astype(f32)
    column = lax.broadcasted_iota(jnp.int32, (size, far_count * padded), 1)
    far = jnp.floor((row + 0.5) * (1.0 / own_rows))
    source = (row + far * (padded - own_rows)).astype(jnp.int32)
    for block in range(block_count):
        kept = (column == source + block * own_rows).astype(f32).astype(bf16)
        held_ref[block * size : (block + 1) * size] = across(kept, held, (1, 0)).astype(bf16)


def fold_kernel(parts_ref, back_ref):
    groups = parts_ref.shape[0]
    far_count = back_ref.shape[0]
    total = sum(parts_ref[group].astype(f32) for group in range(groups))
    wide, narrow = unfold_rows(total, far_count * SLOTS)
    total = jnp.concatenate([wide, narrow], axis=1).astype(bf16)
    order = slot_order(far_count.bit_length() - 1, total.shape[0])
    back_ref[...] = fold_rows(across(order, total, (0, 0)), far_count).astype(bf16)


def held_order(own_rows, cols):
    row = lax.broadcasted_iota(jnp.int32, (cols, cols), 0)
    place = lax.broadcasted_iota(jnp.int32, (1, cols), 1).astype(f32)
    block = jnp.floor((place + 0.5) * (1.0 / own_rows))
    far_count = cols // (2 * own_rows)
    core = (block >= far_count).astype(f32)
    source = place + (block - core * far_count + core - core * far_count) * own_rows
    return (row == source.astype(jnp.int32)).astype(f32).astype(bf16)


def weight_block(weight_ref, part, size):
    columns = []
    for block in range(weight_ref.shape[1] // size):
        pair = [
            weight_ref[part * 2 + core, block * size : (block + 1) * size] for core in range(2)
        ]
        columns.append(jnp.concatenate(pair, axis=0))
    return jnp.concatenate(columns, axis=1)


def class_block(weights_ref, place_ref, cols):
    mine = weights_ref[place_ref[0]]
    both = mine[:, 3 * cols :].astype(f32)
    return both[:, :CLASSES] + both[:, CLASSES : 2 * CLASSES]


def weight_grad_kernel(
    of_other, place_ref, placing_ref, back_ref, mask_ref, features_ref, half_ref
):
    tiles, positions, channels = features_ref.shape
    half = mask_ref.shape[1] // 2
    is_first = place_ref[2] == (1 if of_other else 0)
    back = jnp.concatenate(unfold_rows(back_ref[...].astype(f32), 16), axis=1)
    back = jnp.where(is_first, back[:, :half], back[:, half:]).astype(bf16)
    mask = mask_ref[...].astype(f32)
    mask = jnp.where(is_first, mask[:, :half], mask[:, half:])
    tile_grads = across(placing_ref[...], back, (0, 0))
    spread = jnp.broadcast_to(tile_grads[:, None, :], (tiles, positions, half))
    grad_preact = spread.reshape(tiles * positions, half) * mask
    bias = jnp.sum(grad_preact, axis=0, keepdims=True)
    flattened = features_ref[...].reshape(tiles * positions, channels)
    grad = across(grad_preact.astype(bf16), flattened, (0, 0))
    lanes = channels // half_ref.shape[0]
    bias_rows = jnp.concatenate([bias, jnp.zeros((1, lanes - half), f32)], axis=1)
    bias_rows = jnp.broadcast_to(bias_rows, (8, lanes))
    for place in range(half_ref.shape[0]):
        block = grad[:, place * lanes : (place + 1) * lanes]
        half_ref[place] = jnp.concatenate([block, bias_rows], axis=0).astype(bf16)


def unpack_kernel(parts_ref, grad_ref, bias_ref):
    cores, plane, _, lanes = parts_ref.shape
    half = grad_ref.shape[0] // cores
    biases = []
    for core in range(cores):
        for place in range(plane):
            block = parts_ref[core, place].astype(f32)
            grad_ref[core * half : (core + 1) * half, place * lanes : (place + 1) * lanes] = block[
                :half
            ]
            if place == 0:
                biases.append(block[half : half + 1, :half])
    bias_ref[...] = jnp.concatenate(biases, axis=1)


def run(kernel, name, out_shape, args, specs, scratch=()):
    vmem = pl.BlockSpec(memory_space=pltpu.VMEM)
    smem = pl.BlockSpec(memory_space=pltpu.SMEM)
    kinds = {"v": vmem, "s": smem, "a": pl.BlockSpec(memory_space=pl.ANY)}
    return pl.pallas_call(
        kernel,
        out_shape=out_shape,
        in_specs=[kinds[spec] for spec in specs],
        out_specs=(vmem,) * len(out_shape),
        scratch_shapes=list(scratch),
        compiler_params=pltpu.CompilerParams(vmem_limit_bytes=(56 if scratch else 40) << 20),
        name=name,
    )(*args)


def on_device(
    features,
    tile_slide,
    tile_pos,
    slide_owner,
    slide_label,
    enc_weight,
    enc_bias,
    norm_gain,
    qkv_weight,
    out_weight,
    cls_weight,
):
    far_count = lax.axis_size(FAR)
    near_count = lax.axis_size(NEAR)
    groups = lax.axis_size("x")
    tile_count, _, channels = features.shape
    cols = enc_weight.shape[1]
    emb = cols * groups
    slot_total = far_count * near_count * SLOTS
    group_at = lax.axis_index("x")
    owner_at = lax.axis_index(ENC)

    shape = jax.ShapeDtypeStruct
    place = jnp.stack([group_at, owner_at, lax.axis_index("c")]).astype(jnp.int32)
    width = 3 * cols + 2 * CLASSES

    with jax.named_scope("encode"):
        own_rows = qkv_weight.shape[0]
        width_blocks = width // LANES
        sources = (
            tile_slide.reshape(1, tile_count),
            tile_pos[None, :],
            slide_owner[None, :],
            qkv_weight,
            out_weight,
            cls_weight.T,
            enc_bias[None, :],
            enc_weight.T,
            features,
        )
        send, mask, placing = run(
            send_kernel,
            "send",
            (
                shape((far_count, 24 + held_rows(width_blocks, own_rows), LANES), bf16),
                shape((tile_count * POS, cols), bf16),
                shape((slot_total, tile_count), bf16),
            ),
            (group_at.astype(jnp.int32)[None],) + sources,
            "s" + "a" * len(sources),
            [pltpu.VMEM(source.shape, source.dtype) for source in sources]
            + [pltpu.SemaphoreType.DMA((len(sources),))],
        )

    with jax.named_scope("dispatch"):
        send_near, far_held = run(
            functools.partial(turn_kernel, own_rows),
            "turn",
            (
                shape((groups, near_count, far_count * SLOTS, BLOCK), bf16),
                shape((width_blocks * far_count * own_rows, LANES), bf16),
            ),
            (swap(send, FAR),),
            "v",
        )
        rows = swap(
            send_near.reshape(groups * near_count, far_count * SLOTS, BLOCK), ("x",) + NEAR
        ).reshape(groups, slot_total, BLOCK)

    with jax.named_scope("weights"):
        weights = lax.all_gather(far_held, NEAR, axis=0)

    with jax.named_scope("attend"):
        gain = norm_gain.reshape(groups, 1, cols)
        cls_parts = cls_weight.T.reshape(CLASSES, groups, cols).transpose(1, 0, 2)
        part_logits, att, qkv, ordered = run(
            functools.partial(forward_kernel, own_rows),
            "forward",
            (
                shape((1, CLASSES), f32),
                shape((cols // HD, slot_total, slot_total), f32),
                shape((slot_total, 3 * cols), bf16),
                shape((groups, cols, width), bf16),
            ),
            (place, rows, weights, gain, cls_parts),
            "svvvv",
        )
        all_logits = lax.all_gather(part_logits, "x", axis=0)
        logits, grad_parts = run(
            backward_kernel,
            "backward",
            (
                shape((1, CLASSES), f32),
                shape((groups, near_count, far_count * SLOTS * 3 // 2, LANES), bf16),
            ),
            (
                place,
                all_logits,
                slide_owner[None, :],
                slide_label[None, :],
                rows,
                ordered,
                gain,
                cls_parts,
                att,
                qkv,
            ),
            "svvvvvvvvv",
        )

    with jax.named_scope("give_back"):
        from_near = swap(
            grad_parts.reshape((groups * near_count,) + grad_parts.shape[2:]), ("x",) + NEAR
        ).reshape(grad_parts.shape)
        (folded,) = run(
            fold_kernel, "fold", (shape((far_count, 24, LANES), bf16),), (from_near,), "v"
        )
        back_rows = swap(folded, FAR)

    with jax.named_scope("encoder_grad"):
        plane_count = lax.axis_size(PLANE)
        block = (cols // 2 + 8, channels // plane_count)
        operands = (place, placing, back_rows, mask, features)
        (sent,) = run(
            functools.partial(weight_grad_kernel, True),
            "other_half",
            (shape((plane_count,) + block, bf16),),
            operands,
            "svvvv",
        )
        other = lax.ppermute(sent, "c", [(0, 1), (1, 0)])
        (kept,) = run(
            functools.partial(weight_grad_kernel, False),
            "own_half",
            (shape((plane_count,) + block, bf16),),
            operands,
            "svvvv",
        )

    with jax.named_scope("reduce"):
        core_sum = (kept.astype(f32) + other.astype(f32)).astype(bf16)
        plane_sum = jnp.sum(swap_plane(core_sum).astype(f32), axis=0).astype(bf16)
        total = jnp.sum(gather_copies(plane_sum, "zh").astype(f32), axis=0).astype(bf16)
        copies = jnp.broadcast_to(total[None], (plane_count,) + total.shape)
        all_parts = lax.all_gather(swap_plane(copies), "c", axis=0)
        enc_grad, bias_grad = run(
            unpack_kernel,
            "unpack",
            (shape((cols, channels), f32), shape((1, cols), f32)),
            (all_parts,),
            "v",
        )
    return (logits, enc_grad.T, bias_grad[0])


def solution(mesh):
    enc_count, groups = mesh.devices.shape
    far_count = enc_count // 8
    far_lanes = 4 if far_count >= 16 else far_count // 2
    shape = (4, far_count // far_lanes, far_lanes, 2, groups)
    split = Mesh(mesh.devices.reshape(shape), ENC + ("x",))
    return jax.shard_map(
        on_device,
        mesh=split,
        in_specs=(
            P(ENC, None, None),
            P(ENC, None),
            P(ENC),
            P(),
            P(),
            P(None, "x"),
            P("x"),
            P(),
            P(ENC, None),
            P(ENC, None),
            P(),
        ),
        out_specs=(P(ENC, None), P(None, "x"), P("x")),
        check_vma=False,
    )
```
